1024 devices in a mesh: dp: 16 (over z, core), proto: 64 (over y, x).
Axes of the slice: x: 8, y: 8, z: 8, core: 2. Of those that a mesh axis runs over, the one named last changes fastest.
Arguments:
- student_feat: bfloat16 [12288, 256], P(('dp', 'proto'))
- teacher_feat: bfloat16 [12288, 256], P(('dp', 'proto'))
- prototypes: bfloat16 [65536, 256], P('proto')
- teacher_prototypes: bfloat16 [65536, 256], P('proto')
- live_count: int32 [16], replicated, may hold values from 192 to 768, as said below
Outputs:
- student_grad: float32 [12288, 256], P(('dp', 'proto'))
- proto_grad: float32 [64, 1024, 256], P('proto', 'dp')
The draws below stay inside these ranges and needn't reach their ends.
Inputs may be any that keep to these rules, and one draw needn't show every extreme that they name: `live_count`: some group is full (768 live rows) in every draw; live rows are the first ones of each group.
All inputs are finite; a program needn't handle non-finite values.
Results may differ from the reference program's by a relative error of at most 0.0026.
Values may be sent and summed in bfloat16 or wider, within the bound.
A program may use at most 32 MiB of HBM per device.

```python
import math
import jax
import jax.numpy as jnp
from jax import lax

D = 256
PROTO_DEV = 1024
ITERS = 3
PROTOS = 65536
GROUP_ROWS = 768
ROWS = 12288
N_DP = 16
N_PROTO = 64


def shared_direction(key):
    return jax.random.normal(jax.random.fold_in(key, 11), (D,), jnp.float32) / math.sqrt(D)


def spread_rows(key, count_rows):
    return jax.random.normal(key, (count_rows, D), jnp.float32) / math.sqrt(D)


def banded_coordinate(key, block_count, block_size, center_reach, jitter_reach):
    centers = jax.random.uniform(jax.random.fold_in(key, 1), (block_count,), jnp.float32, -center_reach, center_reach)
    jitter = jax.random.uniform(jax.random.fold_in(key, 2), (block_count, block_size), jnp.float32, -jitter_reach, jitter_reach)
    return (centers[:, None] + jitter).reshape(block_count * block_size, 1)


def proto_base(key):
    direction = shared_direction(key)
    band_key = jax.random.fold_in(key, 21)
    along_axis = banded_coordinate(band_key, PROTOS // PROTO_DEV, PROTO_DEV, 2.5, 0.5)
    return along_axis * direction[None, :] + spread_rows(jax.random.fold_in(key, 22), PROTOS)


def feature_base(key):
    direction = shared_direction(key)
    band_key = jax.random.fold_in(key, 31)
    along_axis = banded_coordinate(band_key, ROWS // GROUP_ROWS, GROUP_ROWS, 2.0, 0.7)
    return along_axis * direction[None, :] + spread_rows(jax.random.fold_in(key, 32), ROWS)


def draw_prototypes(key, part):
    return proto_base(key).astype(jnp.bfloat16)


def draw_teacher_prototypes(key, part):
    jitter = jax.random.normal(jax.random.fold_in(key, 23), (PROTOS, D), jnp.float32) / math.sqrt(D)
    return (proto_base(key) + 0.3 * jitter).astype(jnp.bfloat16)


def draw_student_feat(key, part):
    jitter = jax.random.normal(jax.random.fold_in(key, 33), (ROWS, D), jnp.float32) / math.sqrt(D)
    return (feature_base(key) + 0.3 * jitter).astype(jnp.bfloat16)


def draw_teacher_feat(key, part):
    jitter = jax.random.normal(jax.random.fold_in(key, 34), (ROWS, D), jnp.float32) / math.sqrt(D)
    return (feature_base(key) + 0.3 * jitter).astype(jnp.bfloat16)


def draw_live_count(key, part):
    counts = jax.random.randint(jax.random.fold_in(key, 41), (N_DP,), GROUP_ROWS // 4, GROUP_ROWS + 1)
    full_group = jax.random.randint(jax.random.fold_in(key, 42), (), 0, N_DP)
    return jnp.where(jnp.arange(N_DP) == full_group, GROUP_ROWS, counts).astype(jnp.int32)


def setup_inputs(seed: int = 0) -> dict:
    key_list = jax.random.split(jax.random.key(seed), 6)
    return {
        "student_feat": draw_student_feat(jax.random.fold_in(key_list[5], 71), 0),
        "teacher_feat": draw_teacher_feat(jax.random.fold_in(key_list[5], 71), 0),
        "prototypes": draw_prototypes(jax.random.fold_in(key_list[5], 71), 0),
        "teacher_prototypes": draw_teacher_prototypes(jax.random.fold_in(key_list[5], 71), 0),
        "live_count": draw_live_count(jax.random.fold_in(key_list[5], 71), 0),
    }


student_temp = 0.1
teacher_temp = 0.07
eps_norm = 1e-06

def unit_rows(values):
    widened = values.astype(jnp.float32)
    length = jnp.sqrt(lax.optimization_barrier(jnp.sum(widened * widened, axis=1, keepdims=True)) + eps_norm)
    return (widened / length, length)

def reference(student_feat, teacher_feat, prototypes, teacher_prototypes, live_count):
    student_unit, student_length = unit_rows(student_feat)
    teacher_unit, teacher_length = unit_rows(teacher_feat)
    student_rows = student_unit.astype(jnp.bfloat16)
    teacher_rows = teacher_unit.astype(jnp.bfloat16)
    row_ids = jnp.arange(ROWS, dtype=jnp.int32)
    group_of = (row_ids // GROUP_ROWS).astype(jnp.int32)
    live_mask = row_ids % GROUP_ROWS < live_count[group_of]
    student_blocks = prototypes.reshape(N_PROTO, PROTO_DEV, D)
    teacher_blocks = teacher_prototypes.reshape(N_PROTO, PROTO_DEV, D)

    def teacher_weights(proto_block):
        unit_block, unused_length = unit_rows(proto_block)
        scores = jnp.dot(teacher_rows, unit_block.astype(jnp.bfloat16).T, preferred_element_type=jnp.float32) / teacher_temp
        return jnp.where(live_mask[:, None], jnp.exp(scores), 0.0)

    def student_logits(proto_block):
        unit_block, block_length = unit_rows(proto_block)
        logits = jnp.dot(student_rows, unit_block.astype(jnp.bfloat16).T, preferred_element_type=jnp.float32) / student_temp
        return (logits, unit_block, block_length)
    scale_rows = live_mask.astype(jnp.float32)
    scale_protos = jnp.zeros((N_PROTO, PROTO_DEV), jnp.float32)
    for iteration in range(ITERS):

        def sweep_block(proto_block, current=scale_rows):
            weights = teacher_weights(proto_block)
            inverse = 1.0 / lax.optimization_barrier(jnp.sum(weights * current[:, None], axis=0))
            return (inverse, jnp.dot(weights, inverse, precision=lax.Precision.HIGHEST))
        scale_protos, row_parts = lax.map(sweep_block, teacher_blocks)
        row_sums = lax.optimization_barrier(jnp.sum(row_parts, axis=0))
        scale_rows = jnp.where(live_mask, 1.0 / jnp.where(live_mask, row_sums, 1.0), 0.0)

    def partition_block(proto_block):
        logits, unit_block, block_length = student_logits(proto_block)
        return lax.optimization_barrier(jnp.sum(jnp.exp(logits), axis=1))
    partition = lax.optimization_barrier(jnp.sum(lax.map(partition_block, student_blocks), axis=0))
    log_partition = jnp.log(partition)

    def final_block(carried, inputs):
        student_block, teacher_block, inverse = inputs
        logits, unit_block, block_length = student_logits(student_block)
        targets = teacher_weights(teacher_block) * inverse[None, :] * scale_rows[:, None]
        probs = jnp.exp(logits - log_partition[:, None])
        grad_logits = jnp.where(live_mask[:, None], (probs - targets) / student_temp, 0.0).astype(jnp.bfloat16)
        carried = carried + jnp.dot(grad_logits, unit_block.astype(jnp.bfloat16), preferred_element_type=jnp.float32)
        pushed = jnp.dot(grad_logits.T, student_rows, preferred_element_type=jnp.float32)
        grad_block = (pushed - unit_block * lax.optimization_barrier(jnp.sum(unit_block * pushed, axis=1, keepdims=True))) / block_length
        return (carried, grad_block)
    pulled, grad_blocks = lax.scan(final_block, jnp.zeros((ROWS, D), jnp.float32), (student_blocks, teacher_blocks, scale_protos))
    student_grad = (pulled - student_unit * lax.optimization_barrier(jnp.sum(student_unit * pulled, axis=1, keepdims=True))) / student_length
    return (student_grad, grad_blocks)
```

```python
import jax
import jax.numpy as jnp
from jax import lax
from jax.experimental import pallas as pl
from jax.experimental.pallas import tpu as pltpu
from jax.sharding import PartitionSpec as P

MESH = pl.DeviceIdType.MESH
F32 = jnp.float32
BF16 = jnp.bfloat16

ITERS = 3
EPS = 1e-06
NX = 8
SLOT = 12
HALF = 6
CHUNK = NX * HALF
ROWS = 768
PROTOS = 1024
D = 256
NT = (((1,), (1,)), ((), ()))
TN = (((0,), (0,)), ((), ()))
FAR_FIRST = (4, 3, 5, 2, 6, 1, 7)


def unit_rows(values):
    widened = values.astype(F32)
    length = jnp.sqrt(jnp.sum(widened * widened, axis=1, keepdims=True) + EPS)
    return widened * (1.0 / length), length


def slot_row(index):
    first = index + HALF * ((index * 10923) >> 16)
    rest = index - ROWS // 2
    block = (rest * 1366) >> 16
    inner = rest - block * CHUNK
    six = (inner * 43) >> 8
    second = six * (NX * SLOT) + block * SLOT + HALF + inner - six * HALF
    return jnp.where(index < ROWS // 2, first, second)


def kernel(
    sf, tf, pr, tp, lc, out_s, out_p,
    stage, msg, g1, trow, srow, tpb, prb, wt, ex, gr, ub, ab,
    cs, cr, rs, rr, ps, pg, vv,
    pull, pullb, q1, q2s, q2, push, pushb, sib, zsend, zrecv,
    gsend, grecv, csend, crecv, rsend, rrecv, psend, precv, fsend, frecv,
):
    d = lax.axis_index("dp")
    p = lax.axis_index("proto")
    y, x = p // NX, p % NX
    z, c = d // 2, d % 2

    def xp(k):
        return (d, y * NX + (x + k) % NX)

    def yp(k):
        return (d, ((y + k) % NX) * NX + x)

    def dpp(k):
        return ((d + k) % 16, p)

    def send(src, dst, ssem, rsem, dev):
        pltpu.make_async_remote_copy(
            src_ref=src, dst_ref=dst, send_sem=ssem, recv_sem=rsem, device_id=dev, device_id_type=MESH
        ).start()

    def wait(ref, sem):
        pltpu.make_async_copy(ref, ref, sem).wait()

    barrier = pltpu.get_barrier_semaphore()
    for k in range(1, NX):
        pl.semaphore_signal(barrier, inc=1, device_id=xp(k), device_id_type=MESH)
        pl.semaphore_signal(barrier, inc=1, device_id=yp(k), device_id_type=MESH)
    for k in range(1, 16):
        pl.semaphore_signal(barrier, inc=1, device_id=dpp(k), device_id_type=MESH)

    su, _ = unit_rows(sf[...])
    tu, _ = unit_rows(tf[...])
    stage[...] = jnp.zeros_like(stage)
    stage[0, 0:HALF] = tu[0:HALF]
    stage[0, HALF:SLOT] = su[0:HALF]
    stage[1, 0:HALF] = tu[HALF:SLOT]
    stage[1, HALF:SLOT] = su[HALF:SLOT]
    msg[...] = stage[...].astype(BF16)
    g1[0, x] = msg[0]
    g1[1, y] = msg[1]
    pl.semaphore_wait(barrier, 2 * (NX - 1) + 15)
    for k in FAR_FIRST:
        send(msg.at[0], g1.at[0, x], gsend.at[0], grecv.at[0], xp(k))
        send(msg.at[1], g1.at[1, y], gsend.at[1], grecv.at[1], yp(k))

    def unit_protos(i, carry):
        rows = pl.ds(pl.multiple_of(i * 128, 128), 128)
        tpb[rows, :] = unit_rows(tp[rows, :])[0].astype(BF16)
        prb[rows, :] = unit_rows(pr[rows, :])[0].astype(BF16)
        return carry

    lax.fori_loop(0, PROTOS // 128, unit_protos, 0)
    live = lc[d]
    ub[...] = (slot_row(lax.broadcasted_iota(jnp.int32, (ROWS, 128), 0)) < live).astype(F32)
    flat = lax.broadcasted_iota(jnp.int32, (8, 128), 0) * 128 + lax.broadcasted_iota(jnp.int32, (8, 128), 1)
    live_flat = (slot_row(flat) < live) & (flat < ROWS)

    ri = lax.broadcasted_iota(jnp.int32, (2 * CHUNK, NX * 16), 0)
    ci = lax.broadcasted_iota(jnp.int32, (2 * CHUNK, NX * 16), 1)
    inner = jnp.where(ri < CHUNK, ri, ri - CHUNK)
    six = (inner * 43) >> 8
    source = six * 16 + (inner - six * HALF) + jnp.where(ri < CHUNK, 0, HALF)
    pick = (ci == source).astype(F32).astype(BF16)
    first = pl.ds(pl.multiple_of(y * CHUNK, CHUNK), CHUNK)
    second = pl.ds(pl.multiple_of(ROWS // 2 + x * CHUNK, CHUNK), CHUNK)
    for half, place, peer in ((0, first, yp), (1, second, xp)):
        wait(g1.at[half, pl.ds(0, NX - 1)], grecv.at[half])
        rows = jnp.dot(pick, g1[half].reshape(NX * 16, D), preferred_element_type=F32).astype(BF16)
        trow[place, :] = rows[0:CHUNK]
        srow[place, :] = rows[CHUNK:]
        for k in FAR_FIRST:
            send(trow.at[place], trow.at[place], gsend.at[2 + half], grecv.at[2 + half], peer(k))

    def scores(rows_ref, protos_ref, out_ref, scale):
        for m in range(3):
            for n in range(4):
                rows, cols = pl.ds(m * 256, 256), pl.ds(n * 256, 256)
                s = lax.dot_general(rows_ref[rows, :], protos_ref[cols, :], NT, preferred_element_type=F32)
                out_ref[rows, cols] = jnp.exp(s * scale)

    wait(trow.at[pl.ds(0, 7 * CHUNK)], grecv.at[2])
    wait(trow.at[pl.ds(0, 7 * CHUNK)], grecv.at[3])
    for half, place, peer in ((0, first, yp), (1, second, xp)):
        for k in FAR_FIRST:
            send(srow.at[place], srow.at[place], gsend.at[4 + half], grecv.at[4 + half], peer(k))
    scores(trow, tpb, wt, 1.0 / 0.07)

    def column_pass(it):
        def body(i, acc):
            rows = pl.ds(pl.multiple_of(i * 32, 32), 32)
            w = wt[rows, :]
            u = ub[rows, :]
            for t in range(4):
                ut = jnp.concatenate([u[t * 8 : t * 8 + 8]] * 8, axis=1)
                acc = acc + w[t * 8 : t * 8 + 8] * ut
            return acc

        acc = lax.fori_loop(0, ROWS // 32, body, jnp.zeros((8, PROTOS), F32), unroll=4)
        total = jnp.sum(acc, axis=0, keepdims=True)
        for n in range(8):
            cs[it, n : n + 1, :] = total[:, n * 128 : n * 128 + 128]
        for k in (8, 7, 9, 6, 10, 5, 11, 4, 12, 3, 13, 2, 14, 1, 15):
            send(cs.at[it], cr.at[it, k - 1], csend.at[it], crecv.at[it], dpp(k))

    def column_wait(it):
        wait(cr.at[it], crecv.at[it])
        vv[...] = 1.0 / (cs[it] + jnp.sum(cr[it], axis=0))

    def lane_sums(src_ref, weights, out_ref):
        out_ref[...] = jnp.zeros_like(out_ref)
        for n in range(6):
            rows = pl.ds(n * 128, 128)
            acc = jnp.zeros((128, 128), F32)
            for t in range(8):
                acc = acc + src_ref[rows, pl.ds(t * 128, 128)] * weights[t : t + 1, :]
            out_ref[n : n + 1, :] = jnp.sum(acc.T, axis=0, keepdims=True)

    def spread(flat_rows, out_ref):
        for n in range(6):
            out_ref[pl.ds(n * 128, 128), :] = jnp.broadcast_to(flat_rows[n : n + 1, :], (128, 128)).T

    def proto_send(src, dst, ssem, rsem, axis):
        for k in FAR_FIRST:
            send(src.at[axis], dst.at[axis, k - 1], ssem.at[axis], rsem.at[axis], (xp, yp)[axis](k))

    def proto_sum(src, dst, rsem, axis):
        wait(dst.at[axis], rsem.at[axis])
        return src[axis] + jnp.sum(dst[axis], axis=0)

    def inverse(total):
        return jnp.where(live_flat, 1.0 / jnp.where(live_flat, total, 1.0), 0.0)

    for it in range(ITERS):
        column_pass(it)
        if it == 1:
            wait(srow.at[pl.ds(0, 7 * CHUNK)], grecv.at[4])
            wait(srow.at[pl.ds(0, 7 * CHUNK)], grecv.at[5])
            scores(srow, prb, ex, 10.0)
            lane_sums(ex, jnp.ones((8, 128), F32), ps.at[0])
            proto_send(ps, pg, psend, precv, 0)
        if it == 2:
            ps[1] = proto_sum(ps, pg, precv, 0)
            proto_send(ps, pg, psend, precv, 1)
        column_wait(it)
        src, dst, ssem, rsem = rs.at[it], rr.at[it], rsend.at[it], rrecv.at[it]
        lane_sums(wt, vv[...], src.at[0])
        proto_send(src, dst, ssem, rsem, 0)
        if it == 2:
            partition = proto_sum(ps, pg, precv, 1)
            spread(10.0 * inverse(partition), ab)

            def fold(i, carry):
                rows = pl.ds(pl.multiple_of(i * 32, 32), 32)
                a = ab[rows, :]
                for n in range(8):
                    cols = pl.ds(n * 128, 128)
                    ex[rows, cols] = ex[rows, cols] * a
                    wt[rows, cols] = wt[rows, cols] * vv[n : n + 1, :]
                return carry

            lax.fori_loop(0, ROWS // 32, fold, 0)
        rs[it, 1] = proto_sum(src, dst, rsem, 0)
        proto_send(src, dst, ssem, rsem, 1)
        total = proto_sum(src, dst, rsem, 1)
        spread(inverse(total) * (10.0 if it == ITERS - 1 else 1.0), ub)

    def grads(i, carry):
        rows = pl.ds(pl.multiple_of(i * 32, 32), 32)
        u = ub[rows, :]
        for n in range(8):
            cols = pl.ds(n * 128, 128)
            gr[rows, cols] = (ex[rows, cols] - wt[rows, cols] * u).astype(BF16)
        return carry

    lax.fori_loop(0, ROWS // 32, grads, 0)

    for m in range(3):
        rows = pl.ds(m * 256, 256)
        part = jnp.dot(gr[rows, :], prb[...], preferred_element_type=F32)
        pull[rows, :] = part
        pullb[rows, :] = part.astype(BF16)
    for k in FAR_FIRST:
        to_y = pl.ds(pl.multiple_of(((y + k) % NX) * CHUNK, CHUNK), CHUNK)
        to_x = pl.ds(pl.multiple_of(ROWS // 2 + ((x + k) % NX) * CHUNK, CHUNK), CHUNK)
        send(pullb.at[to_y], q1.at[0, k - 1], fsend.at[0], frecv.at[0], yp(k))
        send(pullb.at[to_x], q1.at[1, k - 1], fsend.at[1], frecv.at[1], xp(k))

    other = pl.ds(pl.multiple_of((1 - c) * 512, 512), 512)
    mine = pl.ds(pl.multiple_of(c * 512, 512), 512)
    pushb[...] = lax.dot_general(gr[:, other], srow[...], TN, preferred_element_type=F32).astype(BF16)
    send(pushb, sib, fsend.at[2], frecv.at[2], (z * 2 + 1 - c, p))
    push[...] = lax.dot_general(gr[:, mine], srow[...], TN, preferred_element_type=F32)
    wait(sib, frecv.at[2])
    zsend[...] = (push[...] + sib[...].astype(F32)).astype(BF16).reshape(8, 64, D)
    keeps = c == z // 4
    for i in range(8):
        to = 8 * c + (i + 2 * z + 8) % 8

        @pl.when(to != d)
        def _(to=to):
            send(zsend.at[to - 8 * c], zrecv.at[z], fsend.at[3], frecv.at[3], (to, p))

    @pl.when(keeps)
    def _():
        zrecv[z] = zsend[d - 8 * c]

    for half, own, peer in ((0, first, xp), (1, second, yp)):
        wait(q1.at[half], frecv.at[half])
        total = pull[own, :] + jnp.sum(q1[half].astype(F32), axis=0)
        for n in range(NX):
            q2s[half, n, 0:HALF] = total[n * HALF : n * HALF + HALF]
            q2s[half, n, HALF:8] = jnp.zeros((8 - HALF, D), F32)
        at = x if half == 0 else y
        for k in FAR_FIRST:
            send(q2s.at[half, (at + k) % NX], q2.at[half, k - 1], fsend.at[4 + half], frecv.at[4 + half], peer(k))

    own_rows = pl.ds(pl.multiple_of(d * 64, 64), 64)
    proto_unit, proto_length = unit_rows(pr[own_rows, :])

    @pl.when(keeps)
    def _():
        wait(zrecv.at[pl.ds(0, 7)], frecv.at[3])
        wait(zrecv.at[pl.ds(0, 7)], fsend.at[3])

    @pl.when(jnp.logical_not(keeps))
    def _():
        wait(zrecv, frecv.at[3])
        wait(zrecv, fsend.at[3])

    pushed = jnp.sum(zrecv[...].astype(F32), axis=0)
    out_p[0] = (pushed - proto_unit * jnp.sum(proto_unit * pushed, axis=1, keepdims=True)) * (1.0 / proto_length)

    student_unit, student_length = unit_rows(sf[...])
    for half in range(2):
        wait(q2.at[half], frecv.at[4 + half])
        at = x if half == 0 else y
        stage[half, 0:8] = q2s[half, at] + jnp.sum(q2[half], axis=0)
    pulled = jnp.concatenate([stage[0, 0:HALF], stage[1, 0:HALF]], axis=0)
    out_s[...] = (pulled - student_unit * jnp.sum(student_unit * pulled, axis=1, keepdims=True)) * (1.0 / student_length)

    for half in range(2):
        wait(g1.at[half, pl.ds(0, NX - 1)], gsend.at[half])
        wait(trow.at[pl.ds(0, 7 * CHUNK)], gsend.at[2 + half])
        wait(srow.at[pl.ds(0, 7 * CHUNK)], gsend.at[4 + half])
        wait(pg.at[half], psend.at[half])
        wait(q1.at[half], fsend.at[half])
        wait(q2.at[half], fsend.at[4 + half])
        for it in range(ITERS):
            wait(rr.at[it, half], rsend.at[it, half])
    for it in range(ITERS):
        wait(cr.at[it], csend.at[it])
    wait(sib, fsend.at[2])


def on_device(student_feat, teacher_feat, prototypes, teacher_prototypes, live_count):
    vmem = pl.BlockSpec(memory_space=pltpu.VMEM)
    dma = pltpu.SemaphoreType.DMA
    return pl.pallas_call(
        kernel,
        out_shape=(
            jax.ShapeDtypeStruct((SLOT, D), F32),
            jax.ShapeDtypeStruct((1, PROTOS // 16, D), F32),
        ),
        in_specs=[vmem, vmem, vmem, vmem, pl.BlockSpec(memory_space=pltpu.SMEM)],
        out_specs=(vmem, vmem),
        scratch_shapes=[
            pltpu.VMEM((2, 16, D), F32),
            pltpu.VMEM((2, 16, D), BF16),
            pltpu.VMEM((2, NX, 16, D), BF16),
            pltpu.VMEM((ROWS, D), BF16),
            pltpu.VMEM((ROWS, D), BF16),
            pltpu.VMEM((PROTOS, D), BF16),
            pltpu.VMEM((PROTOS, D), BF16),
            pltpu.VMEM((ROWS, PROTOS), F32),
            pltpu.VMEM((ROWS, PROTOS), F32),
            pltpu.VMEM((ROWS, PROTOS), BF16),
            pltpu.VMEM((ROWS, 128), F32),
            pltpu.VMEM((ROWS, 128), F32),
            pltpu.VMEM((ITERS, 8, 128), F32),
            pltpu.VMEM((ITERS, 15, 8, 128), F32),
            pltpu.VMEM((ITERS, 2, 8, 128), F32),
            pltpu.VMEM((ITERS, 2, 7, 8, 128), F32),
            pltpu.VMEM((2, 8, 128), F32),
            pltpu.VMEM((2, 7, 8, 128), F32),
            pltpu.VMEM((8, 128), F32),
            pltpu.VMEM((ROWS, D), F32),
            pltpu.VMEM((ROWS, D), BF16),
            pltpu.VMEM((2, 7, CHUNK, D), BF16),
            pltpu.VMEM((2, NX, 8, D), F32),
            pltpu.VMEM((2, 7, 8, D), F32),
            pltpu.VMEM((512, D), F32),
            pltpu.VMEM((512, D), BF16),
            pltpu.VMEM((512, D), BF16),
            pltpu.VMEM((8, 64, D), BF16),
            pltpu.VMEM((8, 64, D), BF16),
            dma((6,)),
            dma((6,)),
            dma((ITERS,)),
            dma((ITERS,)),
            dma((ITERS, 2)),
            dma((ITERS, 2)),
            dma((2,)),
            dma((2,)),
            dma((6,)),
            dma((6,)),
        ],
        compiler_params=pltpu.CompilerParams(
            collective_id=0, has_side_effects=True, vmem_limit_bytes=48 * 1024 * 1024
        ),
    )(student_feat, teacher_feat, prototypes, teacher_prototypes, live_count)


def solution(mesh):
    return jax.shard_map(
        on_device,
        mesh=mesh,
        in_specs=(
            P(("dp", "proto"), None),
            P(("dp", "proto"), None),
            P("proto", None),
            P("proto", None),
            P(),
        ),
        out_specs=(P(("dp", "proto"), None), P("proto", "dp", None)),
        check_vma=False,
    )
```

```python
import jax
import jax.numpy as jnp
from jax import lax
from jax.experimental import pallas as pl
from jax.experimental.pallas import tpu as pltpu
from jax.sharding import PartitionSpec as P

MESH = pl.DeviceIdType.MESH
F32 = jnp.float32
BF16 = jnp.bfloat16

ITERS = 3
EPS = 1e-06
NX = 8
SLOT = 12
HALF = 6
CHUNK = NX * HALF
ROWS = 768
PROTOS = 1024
D = 256
NT = (((1,), (1,)), ((), ()))
TN = (((0,), (0,)), ((), ()))
FAR_FIRST = (4, 3, 5, 2, 6, 1, 7)


def hops(k):
    return min(k % NX, NX - k % NX) + min(k // NX, NX - k // NX)


PLANE = sorted(range(1, NX * NX), key=lambda k: -hops(k))


def unit_rows(values):
    widened = values.astype(F32)
    length = jnp.sqrt(jnp.sum(widened * widened, axis=1, keepdims=True) + EPS)
    return widened * (1.0 / length), length


def slot_row(index):
    first = index + HALF * ((index * 10923) >> 16)
    rest = index - ROWS // 2
    block = (rest * 1366) >> 16
    inner = rest - block * CHUNK
    six = (inner * 43) >> 8
    second = six * (NX * SLOT) + block * SLOT + HALF + inner - six * HALF
    return jnp.where(index < ROWS // 2, first, second)


def kernel(
    sf_hbm, tf_hbm, pr_hbm, tp_hbm, lc_hbm, out_s, out_p,
    sf, tf, pr, tp, lc, isem,
    stage, msg, g1, trow, srow, tpb, prb, wt, ex, gr, ub, ab,
    cs, cr, rs, rr, ps, pg, vv,
    pull, pullb, q1, q2s, q2, sixes, push, pushb, sib, zsend, zrecv,
    gsend, grecv, csend, crecv, rsend, rrecv, psend, precv, fsend, frecv,
):
    d = lax.axis_index("dp")
    p = lax.axis_index("proto")
    y, x = p // NX, p % NX
    z, c = d // 2, d % 2

    def xp(k):
        return (d, y * NX + (x + k) % NX)

    def yp(k):
        return (d, ((y + k) % NX) * NX + x)

    def plane(k):
        return (d, ((y + k // NX) % NX) * NX + (x + k % NX) % NX)

    def dpp(k):
        return ((d + k) % 16, p)

    def send(src, dst, ssem, rsem, dev):
        pltpu.make_async_remote_copy(
            src_ref=src, dst_ref=dst, send_sem=ssem, recv_sem=rsem, device_id=dev, device_id_type=MESH
        ).start()

    def wait(ref, sem):
        pltpu.make_async_copy(ref, ref, sem).wait()

    barrier = pltpu.get_barrier_semaphore()
    for k in PLANE:
        pl.semaphore_signal(barrier, inc=1, device_id=plane(k), device_id_type=MESH)
    for k in range(1, 16):
        pl.semaphore_signal(barrier, inc=1, device_id=dpp(k), device_id_type=MESH)

    inputs = ((tf_hbm, tf), (sf_hbm, sf), (lc_hbm, lc), (tp_hbm, tp), (pr_hbm, pr))
    for i, (src, dst) in enumerate(inputs):
        pltpu.make_async_copy(src, dst, isem.at[i]).start()

    def arrived(i):
        pltpu.make_async_copy(*inputs[i], isem.at[i]).wait()

    arrived(0)
    arrived(1)
    su, _ = unit_rows(sf[...])
    tu, _ = unit_rows(tf[...])
    stage[...] = jnp.zeros_like(stage)
    for kind, unit in enumerate((tu, su)):
        for half in range(2):
            six = unit[half * HALF : half * HALF + HALF]
            stage[kind, half, 0:HALF] = six[:, 0:128]
            stage[kind, half, HALF:SLOT] = six[:, 128:D]
    msg[...] = stage[...].astype(BF16)
    for kind in range(2):
        g1[kind, 0, x] = msg[kind, 0]
        g1[kind, 1, y] = msg[kind, 1]
    pl.semaphore_wait(barrier, NX * NX - 1 + 15)
    for kind in range(2):
        for k in FAR_FIRST:
            for half, at, peer in ((0, x, xp), (1, y, yp)):
                send(
                    msg.at[kind, half], g1.at[kind, half, at],
                    gsend.at[kind * 2 + half], grecv.at[kind * 2 + half], peer(k),
                )

    def unit_protos(i, carry):
        rows = pl.ds(pl.multiple_of(i * 128, 128), 128)
        tpb[rows, :] = unit_rows(tp[rows, :])[0].astype(BF16)
        prb[rows, :] = unit_rows(pr[rows, :])[0].astype(BF16)
        return carry

    arrived(3)
    arrived(4)
    lax.fori_loop(0, PROTOS // 128, unit_protos, 0)
    arrived(2)
    live = lc[d]
    ub[...] = (slot_row(lax.broadcasted_iota(jnp.int32, (ROWS, 128), 0)) < live).astype(F32)
    flat = lax.broadcasted_iota(jnp.int32, (6, 128), 0) * 128 + lax.broadcasted_iota(jnp.int32, (6, 128), 1)
    live_flat = slot_row(flat) < live

    ri = lax.broadcasted_iota(jnp.int32, (2 * CHUNK, NX * 16), 0)
    ci = lax.broadcasted_iota(jnp.int32, (2 * CHUNK, NX * 16), 1)
    inner = jnp.where(ri < CHUNK, ri, ri - CHUNK)
    six = (inner * 43) >> 8
    source = six * 16 + (inner - six * HALF) + jnp.where(ri < CHUNK, 0, HALF)
    pick = (ci == source).astype(F32).astype(BF16)
    first = pl.ds(pl.multiple_of(y * CHUNK, CHUNK), CHUNK)
    second = pl.ds(pl.multiple_of(ROWS // 2 + x * CHUNK, CHUNK), CHUNK)

    def second_gather(kind, rows_ref):
        for half, place, peer in ((0, first, yp), (1, second, xp)):
            wait(g1.at[kind, half, pl.ds(0, NX - 1)], grecv.at[kind * 2 + half])
            picked = jnp.dot(pick, g1[kind, half].reshape(NX * 16, 128), preferred_element_type=F32).astype(BF16)
            rows_ref[place, 0:128] = picked[0:CHUNK]
            rows_ref[place, 128:D] = picked[CHUNK:]
            for k in FAR_FIRST:
                sem = 4 + kind * 2 + half
                send(rows_ref.at[place], rows_ref.at[place], gsend.at[sem], grecv.at[sem], peer(k))

    second_gather(0, trow)

    def scores(rows_ref, protos_ref, out_ref, scale):
        for m in range(3):
            for n in range(4):
                rows, cols = pl.ds(m * 256, 256), pl.ds(n * 256, 256)
                s = lax.dot_general(rows_ref[rows, :], protos_ref[cols, :], NT, preferred_element_type=F32)
                out_ref[rows, cols] = jnp.exp(s * scale)

    wait(trow.at[pl.ds(0, 7 * CHUNK)], grecv.at[4])
    wait(trow.at[pl.ds(0, 7 * CHUNK)], grecv.at[5])
    second_gather(1, srow)
    scores(trow, tpb, wt, 1.0 / 0.07)

    def column_pass(it):
        def body(i, acc):
            rows = pl.ds(pl.multiple_of(i * 32, 32), 32)
            w = wt[rows, :]
            u = ub[rows, :]
            for t in range(4):
                ut = jnp.concatenate([u[t * 8 : t * 8 + 8]] * 8, axis=1)
                acc = acc + w[t * 8 : t * 8 + 8] * ut
            return acc

        acc = lax.fori_loop(0, ROWS // 32, body, jnp.zeros((8, PROTOS), F32), unroll=4)
        total = jnp.sum(acc, axis=0, keepdims=True)
        for n in range(8):
            cs[it, n : n + 1, :] = total[:, n * 128 : n * 128 + 128]
        for k in (8, 7, 9, 6, 10, 5, 11, 4, 12, 3, 13, 2, 14, 1, 15):
            send(cs.at[it], cr.at[it, k - 1], csend.at[it], crecv.at[it], dpp(k))

    def column_wait(it):
        wait(cr.at[it], crecv.at[it])
        vv[...] = 1.0 / (cs[it] + jnp.sum(cr[it], axis=0))

    def lane_sums(src_ref, weights, out_ref):
        for n in range(6):
            rows = pl.ds(n * 128, 128)
            acc = jnp.zeros((128, 128), F32)
            for t in range(8):
                acc = acc + src_ref[rows, pl.ds(t * 128, 128)] * weights[t : t + 1, :]
            out_ref[n : n + 1, :] = jnp.sum(acc.T, axis=0, keepdims=True)

    def spread(flat_rows, out_ref):
        for n in range(6):
            out_ref[pl.ds(n * 128, 128), :] = jnp.broadcast_to(flat_rows[n : n + 1, :], (128, 128)).T

    def proto_send(src, dst, ssem, rsem, axis):
        for k in FAR_FIRST:
            send(src.at[axis], dst.at[axis, k - 1], ssem.at[axis], rsem.at[axis], (xp, yp)[axis](k))

    def proto_sum(src, dst, rsem, axis):
        wait(dst.at[axis], rsem.at[axis])
        return src[axis] + jnp.sum(dst[axis], axis=0)

    def inverse(total):
        return jnp.where(live_flat, 1.0 / jnp.where(live_flat, total, 1.0), 0.0)

    for it in range(ITERS):
        column_pass(it)
        if it == 1:
            wait(srow.at[pl.ds(0, 7 * CHUNK)], grecv.at[6])
            wait(srow.at[pl.ds(0, 7 * CHUNK)], grecv.at[7])
            scores(srow, prb, ex, 10.0)
            lane_sums(ex, jnp.ones((8, 128), F32), ps.at[0])
            proto_send(ps, pg, psend, precv, 0)
        if it == 2:
            ps[1] = proto_sum(ps, pg, precv, 0)
            proto_send(ps, pg, psend, precv, 1)
        column_wait(it)
        lane_sums(wt, vv[...], rs.at[it])
        for k in PLANE:
            send(rs.at[it], rr.at[it, k - 1], rsend.at[it], rrecv.at[it], plane(k))
        if it == 2:
            partition = proto_sum(ps, pg, precv, 1)
            spread(10.0 * inverse(partition), ab)

            def fold(i, carry):
                rows = pl.ds(pl.multiple_of(i * 32, 32), 32)
                a = ab[rows, :]
                for n in range(8):
                    cols = pl.ds(n * 128, 128)
                    ex[rows, cols] = ex[rows, cols] * a
                    wt[rows, cols] = wt[rows, cols] * vv[n : n + 1, :]
                return carry

            lax.fori_loop(0, ROWS // 32, fold, 0)
        wait(rr.at[it], rrecv.at[it])
        total = rs[it] + jnp.sum(rr[it], axis=0)
        spread(inverse(total) * (10.0 if it == ITERS - 1 else 1.0), ub)

    def grads(i, carry):
        rows = pl.ds(pl.multiple_of(i * 32, 32), 32)
        u = ub[rows, :]
        for n in range(8):
            cols = pl.ds(n * 128, 128)
            gr[rows, cols] = (ex[rows, cols] - wt[rows, cols] * u).astype(BF16)
        return carry

    lax.fori_loop(0, ROWS // 32, grads, 0)

    for m in range(3):
        rows = pl.ds(m * 256, 256)
        part = jnp.dot(gr[rows, :], prb[...], preferred_element_type=F32)
        pull[rows, :] = part
        pullb[rows, :] = part.astype(BF16)
    for k in FAR_FIRST:
        to_y = pl.ds(pl.multiple_of(((y + k) % NX) * CHUNK, CHUNK), CHUNK)
        to_x = pl.ds(pl.multiple_of(ROWS // 2 + ((x + k) % NX) * CHUNK, CHUNK), CHUNK)
        send(pullb.at[to_y], q1.at[0, k - 1], fsend.at[0], frecv.at[0], yp(k))
        send(pullb.at[to_x], q1.at[1, k - 1], fsend.at[1], frecv.at[1], xp(k))

    other = pl.ds(pl.multiple_of((1 - c) * 512, 512), 512)
    mine = pl.ds(pl.multiple_of(c * 512, 512), 512)
    pushb[...] = lax.dot_general(gr[:, other], srow[...], TN, preferred_element_type=F32).astype(BF16)
    send(pushb, sib, fsend.at[2], frecv.at[2], (z * 2 + 1 - c, p))
    push[...] = lax.dot_general(gr[:, mine], srow[...], TN, preferred_element_type=F32)
    wait(sib, frecv.at[2])
    zsend[...] = (push[...] + sib[...].astype(F32)).astype(BF16).reshape(8, 64, D)
    keeps = c == z // 4
    for k in FAR_FIRST + (0,):
        for core in range(2):
            to = ((z + k) % NX) * 2 + core

            @pl.when((to // 8 == c) & (to != d))
            def _(to=to):
                send(zsend.at[to - 8 * c], zrecv.at[z], fsend.at[3], frecv.at[3], (to, p))

    @pl.when(keeps)
    def _():
        zrecv[z] = zsend[d - 8 * c]

    for half, own, peer in ((0, first, xp), (1, second, yp)):
        wait(q1.at[half], frecv.at[half])
        total = pull[own, :] + jnp.sum(q1[half].astype(F32), axis=0)
        for n in range(NX):
            q2s[half, n, 0:HALF] = total[n * HALF : n * HALF + HALF]
            q2s[half, n, HALF:8] = jnp.zeros((8 - HALF, D), F32)
        at = x if half == 0 else y
        for k in FAR_FIRST:
            send(q2s.at[half, (at + k) % NX], q2.at[half, k - 1], fsend.at[4 + half], frecv.at[4 + half], peer(k))

    own_rows = pl.ds(pl.multiple_of(d * 64, 64), 64)
    proto_unit, proto_length = unit_rows(pr[own_rows, :])

    @pl.when(keeps)
    def _():
        wait(zrecv.at[pl.ds(0, 7)], frecv.at[3])
        wait(zrecv.at[pl.ds(0, 7)], fsend.at[3])

    @pl.when(jnp.logical_not(keeps))
    def _():
        wait(zrecv, frecv.at[3])
        wait(zrecv, fsend.at[3])

    pushed = jnp.sum(zrecv[...].astype(F32), axis=0)
    out_p[0] = (pushed - proto_unit * jnp.sum(proto_unit * pushed, axis=1, keepdims=True)) * (1.0 / proto_length)

    student_unit, student_length = unit_rows(sf[...])
    for half in range(2):
        wait(q2.at[half], frecv.at[4 + half])
        at = x if half == 0 else y
        sixes[half] = q2s[half, at] + jnp.sum(q2[half], axis=0)
    pulled = jnp.concatenate([sixes[0, 0:HALF], sixes[1, 0:HALF]], axis=0)
    out_s[...] = (pulled - student_unit * jnp.sum(student_unit * pulled, axis=1, keepdims=True)) * (1.0 / student_length)

    for half in range(2):
        for kind, rows_ref in enumerate((trow, srow)):
            wait(g1.at[kind, half, pl.ds(0, NX - 1)], gsend.at[kind * 2 + half])
            wait(rows_ref.at[pl.ds(0, 7 * CHUNK)], gsend.at[4 + kind * 2 + half])
        wait(pg.at[half], psend.at[half])
        wait(q1.at[half], fsend.at[half])
        wait(q2.at[half], fsend.at[4 + half])
    for it in range(ITERS):
        wait(rr.at[it], rsend.at[it])
        wait(cr.at[it], csend.at[it])
    wait(sib, fsend.at[2])


def on_device(student_feat, teacher_feat, prototypes, teacher_prototypes, live_count):
    vmem = pl.BlockSpec(memory_space=pltpu.VMEM)
    dma = pltpu.SemaphoreType.DMA
    return pl.pallas_call(
        kernel,
        out_shape=(
            jax.ShapeDtypeStruct((SLOT, D), F32),
            jax.ShapeDtypeStruct((1, PROTOS // 16, D), F32),
        ),
        in_specs=[pl.BlockSpec(memory_space=pl.ANY)] * 5,
        out_specs=(vmem, vmem),
        scratch_shapes=[
            pltpu.VMEM((SLOT, D), BF16),
            pltpu.VMEM((SLOT, D), BF16),
            pltpu.VMEM((PROTOS, D), BF16),
            pltpu.VMEM((PROTOS, D), BF16),
            pltpu.SMEM((16,), jnp.int32),
            dma((5,)),
            pltpu.VMEM((2, 2, 16, 128), F32),
            pltpu.VMEM((2, 2, 16, 128), BF16),
            pltpu.VMEM((2, 2, NX, 16, 128), BF16),
            pltpu.VMEM((ROWS, D), BF16),
            pltpu.VMEM((ROWS, D), BF16),
            pltpu.VMEM((PROTOS, D), BF16),
            pltpu.VMEM((PROTOS, D), BF16),
            pltpu.VMEM((ROWS, PROTOS), F32),
            pltpu.VMEM((ROWS, PROTOS), F32),
            pltpu.VMEM((ROWS, PROTOS), BF16),
            pltpu.VMEM((ROWS, 128), F32),
            pltpu.VMEM((ROWS, 128), F32),
            pltpu.VMEM((ITERS, 8, 128), F32),
            pltpu.VMEM((ITERS, 15, 8, 128), F32),
            pltpu.VMEM((ITERS, 6, 128), F32),
            pltpu.VMEM((ITERS, 63, 6, 128), F32),
            pltpu.VMEM((2, 6, 128), F32),
            pltpu.VMEM((2, 7, 6, 128), F32),
            pltpu.VMEM((8, 128), F32),
            pltpu.VMEM((ROWS, D), F32),
            pltpu.VMEM((ROWS, D), BF16),
            pltpu.VMEM((2, 7, CHUNK, D), BF16),
            pltpu.VMEM((2, NX, 8, D), F32),
            pltpu.VMEM((2, 7, 8, D), F32),
            pltpu.VMEM((2, 8, D), F32),
            pltpu.VMEM((512, D), F32),
            pltpu.VMEM((512, D), BF16),
            pltpu.VMEM((512, D), BF16),
            pltpu.VMEM((8, 64, D), BF16),
            pltpu.VMEM((8, 64, D), BF16),
            dma((8,)),
            dma((8,)),
            dma((ITERS,)),
            dma((ITERS,)),
            dma((ITERS,)),
            dma((ITERS,)),
            dma((2,)),
            dma((2,)),
            dma((6,)),
            dma((6,)),
        ],
        compiler_params=pltpu.CompilerParams(
            collective_id=0, has_side_effects=True, vmem_limit_bytes=60 * 1024 * 1024
        ),
    )(student_feat, teacher_feat, prototypes, teacher_prototypes, live_count)


def solution(mesh):
    return jax.shard_map(
        on_device,
        mesh=mesh,
        in_specs=(
            P(("dp", "proto"), None),
            P(("dp", "proto"), None),
            P("proto", None),
            P("proto", None),
            P(),
        ),
        out_specs=(P(("dp", "proto"), None), P("proto", "dp", None)),
        check_vma=False,
    )
```

```python
import jax
import jax.numpy as jnp
from jax import lax
from jax.experimental import pallas as pl
from jax.experimental.pallas import tpu as pltpu
from jax.sharding import PartitionSpec as P

MESH = pl.DeviceIdType.MESH
F32 = jnp.float32
BF16 = jnp.bfloat16

ITERS = 3
EPS = 1e-06
NX = 8
SLOT = 12
HALF = 6
CHUNK = NX * HALF
ROWS = 768
PROTOS = 1024
D = 256
NT = (((1,), (1,)), ((), ()))
TN = (((0,), (0,)), ((), ()))
FAR_FIRST = (4, 3, 5, 2, 6, 1, 7)


def hops(k):
    return min(k % NX, NX - k % NX) + min(k // NX, NX - k // NX)


PLANE = sorted(range(1, NX * NX), key=lambda k: -hops(k))


def unit_rows(values):
    widened = values.astype(F32)
    length = jnp.sqrt(jnp.sum(widened * widened, axis=1, keepdims=True) + EPS)
    return widened * (1.0 / length), length


def slot_row(index):
    first = index + HALF * ((index * 10923) >> 16)
    rest = index - ROWS // 2
    block = (rest * 1366) >> 16
    inner = rest - block * CHUNK
    six = (inner * 43) >> 8
    second = six * (NX * SLOT) + block * SLOT + HALF + inner - six * HALF
    return jnp.where(index < ROWS // 2, first, second)


def kernel(
    sf_hbm, tf_hbm, pr_hbm, tp_hbm, lc_hbm, out_s, out_p,
    sf, tf, pr, tp, lc, isem,
    stage, msg, g1, trow, srow, tpb, prb, wt, ex, gr, ub, ab,
    cs, cr, rs, rr, ps, pg, vv,
    pull, pullw, pullb, q1, q2s, q2, sixes, push, pushb, sib, zsend, zrecv,
    gsend, grecv, csend, crecv, rsend, rrecv, psend, precv, fsend, frecv,
):
    d = lax.axis_index("dp")
    p = lax.axis_index("proto")
    y, x = p // NX, p % NX
    z, c = d // 2, d % 2

    def xp(k):
        return (d, y * NX + (x + k) % NX)

    def yp(k):
        return (d, ((y + k) % NX) * NX + x)

    def plane(k):
        return (d, ((y + k // NX) % NX) * NX + (x + k % NX) % NX)

    def dpp(k):
        return ((d + k) % 16, p)

    def send(src, dst, ssem, rsem, dev):
        pltpu.make_async_remote_copy(
            src_ref=src, dst_ref=dst, send_sem=ssem, recv_sem=rsem, device_id=dev, device_id_type=MESH
        ).start()

    def wait(ref, sem):
        pltpu.make_async_copy(ref, ref, sem).wait()

    barrier = pltpu.get_barrier_semaphore()
    for k in PLANE:
        pl.semaphore_signal(barrier, inc=1, device_id=plane(k), device_id_type=MESH)
    for k in range(1, 16):
        pl.semaphore_signal(barrier, inc=1, device_id=dpp(k), device_id_type=MESH)

    inputs = ((tf_hbm, tf), (sf_hbm, sf), (lc_hbm, lc), (tp_hbm, tp), (pr_hbm, pr))
    for i, (src, dst) in enumerate(inputs):
        pltpu.make_async_copy(src, dst, isem.at[i]).start()

    def arrived(i):
        pltpu.make_async_copy(*inputs[i], isem.at[i]).wait()

    arrived(0)
    arrived(1)
    su, _ = unit_rows(sf[...])
    tu, _ = unit_rows(tf[...])
    stage[...] = jnp.zeros_like(stage)
    for kind, unit in enumerate((tu, su)):
        for half in range(2):
            six = unit[half * HALF : half * HALF + HALF]
            stage[kind, half, 0:HALF] = six[:, 0:128]
            stage[kind, half, HALF:SLOT] = six[:, 128:D]
    msg[...] = stage[...].astype(BF16)
    for kind in range(2):
        g1[kind, 0, x] = msg[kind, 0]
        g1[kind, 1, y] = msg[kind, 1]
    pl.semaphore_wait(barrier, NX * NX - 1 + 15)
    for kind in range(2):
        for k in FAR_FIRST:
            for half, at, peer in ((0, x, xp), (1, y, yp)):
                send(
                    msg.at[kind, half], g1.at[kind, half, at],
                    gsend.at[kind * 2 + half], grecv.at[kind * 2 + half], peer(k),
                )

    def unit_protos(i, carry):
        rows = pl.ds(pl.multiple_of(i * 128, 128), 128)
        tpb[rows, :] = unit_rows(tp[rows, :])[0].astype(BF16)
        prb[rows, :] = unit_rows(pr[rows, :])[0].astype(BF16)
        return carry

    arrived(3)
    arrived(4)
    lax.fori_loop(0, PROTOS // 128, unit_protos, 0)
    arrived(2)
    live = lc[d]
    ub[...] = (slot_row(lax.broadcasted_iota(jnp.int32, (ROWS, 128), 0)) < live).astype(F32)
    flat = lax.broadcasted_iota(jnp.int32, (6, 128), 0) * 128 + lax.broadcasted_iota(jnp.int32, (6, 128), 1)
    live_flat = slot_row(flat) < live

    ri = lax.broadcasted_iota(jnp.int32, (2 * CHUNK, NX * 16), 0)
    ci = lax.broadcasted_iota(jnp.int32, (2 * CHUNK, NX * 16), 1)
    inner = jnp.where(ri < CHUNK, ri, ri - CHUNK)
    six = (inner * 43) >> 8
    source = six * 16 + (inner - six * HALF) + jnp.where(ri < CHUNK, 0, HALF)
    pick = (ci == source).astype(F32).astype(BF16)
    first = pl.ds(pl.multiple_of(y * CHUNK, CHUNK), CHUNK)
    second = pl.ds(pl.multiple_of(ROWS // 2 + x * CHUNK, CHUNK), CHUNK)

    def second_gather(kind, rows_ref):
        for half, place, peer in ((0, first, yp), (1, second, xp)):
            wait(g1.at[kind, half, pl.ds(0, NX - 1)], grecv.at[kind * 2 + half])
            picked = jnp.dot(pick, g1[kind, half].reshape(NX * 16, 128), preferred_element_type=F32).astype(BF16)
            rows_ref[place, 0:128] = picked[0:CHUNK]
            rows_ref[place, 128:D] = picked[CHUNK:]
            for k in FAR_FIRST:
                sem = 4 + kind * 2 + half
                send(rows_ref.at[place], rows_ref.at[place], gsend.at[sem], grecv.at[sem], peer(k))

    second_gather(0, trow)

    def scores(rows_ref, protos_ref, out_ref, scale, weighted=False):
        parts = []
        for n in range(4):
            acc = jnp.zeros((8, 256), F32)
            for m in range(3):
                rows, cols = pl.ds(m * 256, 256), pl.ds(n * 256, 256)
                s = lax.dot_general(rows_ref[rows, :], protos_ref[cols, :], NT, preferred_element_type=F32)
                e = jnp.exp(s * scale)
                out_ref[rows, cols] = e
                if weighted:
                    u = jnp.concatenate([ub[rows, :]] * 2, axis=1)
                    acc = acc + jnp.sum((e * u).reshape(32, 8, 256), axis=0)
            parts.append(acc)
        return jnp.concatenate(parts, axis=1)

    wait(trow.at[pl.ds(0, 7 * CHUNK)], grecv.at[4])
    wait(trow.at[pl.ds(0, 7 * CHUNK)], grecv.at[5])
    second_gather(1, srow)
    first_sums = scores(trow, tpb, wt, 1.0 / 0.07, True)

    def column_pass(it):
        def body(i, acc):
            rows = pl.ds(pl.multiple_of(i * 32, 32), 32)
            w = wt[rows, :]
            u = ub[rows, :]
            for t in range(4):
                ut = jnp.concatenate([u[t * 8 : t * 8 + 8]] * 8, axis=1)
                acc = acc + w[t * 8 : t * 8 + 8] * ut
            return acc

        if it == 0:
            acc = first_sums
        else:
            acc = lax.fori_loop(0, ROWS // 32, body, jnp.zeros((8, PROTOS), F32), unroll=4)
        total = jnp.sum(acc, axis=0, keepdims=True)
        for n in range(8):
            cs[it, n : n + 1, :] = total[:, n * 128 : n * 128 + 128]
        for k in (8, 7, 9, 6, 10, 5, 11, 4, 12, 3, 13, 2, 14, 1, 15):
            send(cs.at[it], cr.at[it, k - 1], csend.at[it], crecv.at[it], dpp(k))

    def column_wait(it):
        wait(cr.at[it], crecv.at[it])
        vv[...] = 1.0 / (cs[it] + jnp.sum(cr[it], axis=0))

    def lane_sums(src_ref, weights, out_ref):
        for n in range(6):
            rows = pl.ds(n * 128, 128)
            acc = jnp.zeros((128, 128), F32)
            for t in range(8):
                acc = acc + src_ref[rows, pl.ds(t * 128, 128)] * weights[t : t + 1, :]
            out_ref[n : n + 1, :] = jnp.sum(acc.T, axis=0, keepdims=True)

    def spread(flat_rows, out_ref):
        for n in range(6):
            out_ref[pl.ds(n * 128, 128), :] = jnp.broadcast_to(flat_rows[n : n + 1, :], (128, 128)).T

    def proto_send(src, dst, ssem, rsem, axis):
        for k in FAR_FIRST:
            send(src.at[axis], dst.at[axis, k - 1], ssem.at[axis], rsem.at[axis], (xp, yp)[axis](k))

    def proto_sum(src, dst, rsem, axis):
        wait(dst.at[axis], rsem.at[axis])
        return src[axis] + jnp.sum(dst[axis], axis=0)

    def inverse(total):
        return jnp.where(live_flat, 1.0 / jnp.where(live_flat, total, 1.0), 0.0)

    for it in range(ITERS):
        column_pass(it)
        if it == 1:
            wait(srow.at[pl.ds(0, 7 * CHUNK)], grecv.at[6])
            wait(srow.at[pl.ds(0, 7 * CHUNK)], grecv.at[7])
            scores(srow, prb, ex, 10.0)
            lane_sums(ex, jnp.ones((8, 128), F32), ps.at[0])
            proto_send(ps, pg, psend, precv, 0)
        if it == 2:
            ps[1] = proto_sum(ps, pg, precv, 0)
            proto_send(ps, pg, psend, precv, 1)
        column_wait(it)
        lane_sums(wt, vv[...], rs.at[it])
        for k in PLANE:
            send(rs.at[it], rr.at[it, k - 1], rsend.at[it], rrecv.at[it], plane(k))
        if it == 2:
            partition = proto_sum(ps, pg, precv, 1)
            spread(10.0 * inverse(partition), ab)

            v_row = jnp.concatenate([vv[n : n + 1, :] for n in range(8)], axis=1)

            def by_protos(values):
                high = values.astype(BF16)
                low = (values - high.astype(F32)).astype(BF16)
                return jnp.dot(high, prb[...], preferred_element_type=F32) + jnp.dot(
                    low, prb[...], preferred_element_type=F32
                )

            def fold(i, carry):
                rows = pl.ds(pl.multiple_of(i * 128, 128), 128)
                e = ex[rows, :] * jnp.concatenate([ab[rows, :]] * 8, axis=1)
                ex[rows, :] = e
                pull[rows, :] = by_protos(e)
                w = wt[rows, :] * v_row
                wt[rows, :] = w
                pullw[rows, :] = by_protos(w)
                return carry

            lax.fori_loop(0, ROWS // 128, fold, 0)
        wait(rr.at[it], rrecv.at[it])
        total = rs[it] + jnp.sum(rr[it], axis=0)
        spread(inverse(total) * (10.0 if it == ITERS - 1 else 1.0), ub)

    def finish(i, carry):
        rows = pl.ds(pl.multiple_of(i * 48, 48), 48)
        u = jnp.concatenate([ub[rows, :]] * 2, axis=1)
        part = pull[rows, :] - pullw[rows, :] * u
        pull[rows, :] = part
        pullb[rows, :] = part.astype(BF16)
        return carry

    lax.fori_loop(0, ROWS // 48, finish, 0, unroll=2)
    for k in FAR_FIRST:
        to_y = pl.ds(pl.multiple_of(((y + k) % NX) * CHUNK, CHUNK), CHUNK)
        to_x = pl.ds(pl.multiple_of(ROWS // 2 + ((x + k) % NX) * CHUNK, CHUNK), CHUNK)
        send(pullb.at[to_y], q1.at[0, k - 1], fsend.at[0], frecv.at[0], yp(k))
        send(pullb.at[to_x], q1.at[1, k - 1], fsend.at[1], frecv.at[1], xp(k))

    other = pl.ds(pl.multiple_of((1 - c) * 512, 512), 512)
    mine = pl.ds(pl.multiple_of(c * 512, 512), 512)

    def grads(first):
        def body(i, carry):
            rows = pl.ds(pl.multiple_of(i * 32, 32), 32)
            u = ub[rows, :]
            for n in range(4):
                cols = pl.ds(pl.multiple_of(first + n * 128, 128), 128)
                gr[rows, cols] = (ex[rows, cols] - wt[rows, cols] * u).astype(BF16)
            return carry

        lax.fori_loop(0, ROWS // 32, body, 0, unroll=2)

    grads((1 - c) * 512)
    pushb[...] = lax.dot_general(gr[:, other], srow[...], TN, preferred_element_type=F32).astype(BF16)
    send(pushb, sib, fsend.at[2], frecv.at[2], (z * 2 + 1 - c, p))
    grads(c * 512)
    push[...] = lax.dot_general(gr[:, mine], srow[...], TN, preferred_element_type=F32)
    wait(sib, frecv.at[2])
    zsend[...] = (push[...] + sib[...].astype(F32)).astype(BF16).reshape(8, 64, D)
    keeps = c == z // 4
    for k in FAR_FIRST + (0,):
        for core in range(2):
            to = ((z + k) % NX) * 2 + core

            @pl.when((to // 8 == c) & (to != d))
            def _(to=to):
                send(zsend.at[to - 8 * c], zrecv.at[z], fsend.at[3], frecv.at[3], (to, p))

    @pl.when(keeps)
    def _():
        zrecv[z] = zsend[d - 8 * c]

    for half, own, peer in ((0, first, xp), (1, second, yp)):
        wait(q1.at[half], frecv.at[half])
        total = pull[own, :] + jnp.sum(q1[half].astype(F32), axis=0)
        for n in range(NX):
            q2s[half, n, 0:HALF] = total[n * HALF : n * HALF + HALF]
            q2s[half, n, HALF:8] = jnp.zeros((8 - HALF, D), F32)
        at = x if half == 0 else y
        for k in FAR_FIRST:
            send(q2s.at[half, (at + k) % NX], q2.at[half, k - 1], fsend.at[4 + half], frecv.at[4 + half], peer(k))

    own_rows = pl.ds(pl.multiple_of(d * 64, 64), 64)
    proto_unit, proto_length = unit_rows(pr[own_rows, :])

    @pl.when(keeps)
    def _():
        wait(zrecv.at[pl.ds(0, 7)], frecv.at[3])
        wait(zrecv.at[pl.ds(0, 7)], fsend.at[3])

    @pl.when(jnp.logical_not(keeps))
    def _():
        wait(zrecv, frecv.at[3])
        wait(zrecv, fsend.at[3])

    pushed = jnp.sum(zrecv[...].astype(F32), axis=0)
    out_p[0] = (pushed - proto_unit * jnp.sum(proto_unit * pushed, axis=1, keepdims=True)) * (1.0 / proto_length)

    student_unit, student_length = unit_rows(sf[...])
    for half in range(2):
        wait(q2.at[half], frecv.at[4 + half])
        at = x if half == 0 else y
        sixes[half] = q2s[half, at] + jnp.sum(q2[half], axis=0)
    pulled = jnp.concatenate([sixes[0, 0:HALF], sixes[1, 0:HALF]], axis=0)
    out_s[...] = (pulled - student_unit * jnp.sum(student_unit * pulled, axis=1, keepdims=True)) * (1.0 / student_length)

    for half in range(2):
        for kind, rows_ref in enumerate((trow, srow)):
            wait(g1.at[kind, half, pl.ds(0, NX - 1)], gsend.at[kind * 2 + half])
            wait(rows_ref.at[pl.ds(0, 7 * CHUNK)], gsend.at[4 + kind * 2 + half])
        wait(pg.at[half], psend.at[half])
        wait(q1.at[half], fsend.at[half])
        wait(q2.at[half], fsend.at[4 + half])
    for it in range(ITERS):
        wait(rr.at[it], rsend.at[it])
        wait(cr.at[it], csend.at[it])
    wait(sib, fsend.at[2])


def on_device(*arguments):
    vmem = pl.BlockSpec(memory_space=pltpu.VMEM)
    dma = pltpu.SemaphoreType.DMA
    return pl.pallas_call(
        kernel,
        out_shape=(
            jax.ShapeDtypeStruct((SLOT, D), F32),
            jax.ShapeDtypeStruct((1, PROTOS // 16, D), F32),
        ),
        in_specs=[pl.BlockSpec(memory_space=pltpu.HBM)] * 5,
        out_specs=(vmem, vmem),
        scratch_shapes=[
            pltpu.VMEM((SLOT, D), BF16),
            pltpu.VMEM((SLOT, D), BF16),
            pltpu.VMEM((PROTOS, D), BF16),
            pltpu.VMEM((PROTOS, D), BF16),
            pltpu.SMEM((16,), jnp.int32),
            dma((5,)),
            pltpu.VMEM((2, 2, 16, 128), F32),
            pltpu.VMEM((2, 2, 16, 128), BF16),
            pltpu.VMEM((2, 2, NX, 16, 128), BF16),
            pltpu.VMEM((ROWS, D), BF16),
            pltpu.VMEM((ROWS, D), BF16),
            pltpu.VMEM((PROTOS, D), BF16),
            pltpu.VMEM((PROTOS, D), BF16),
            pltpu.VMEM((ROWS, PROTOS), F32),
            pltpu.VMEM((ROWS, PROTOS), F32),
            pltpu.VMEM((ROWS, PROTOS), BF16),
            pltpu.VMEM((ROWS, 128), F32),
            pltpu.VMEM((ROWS, 128), F32),
            pltpu.VMEM((ITERS, 8, 128), F32),
            pltpu.VMEM((ITERS, 15, 8, 128), F32),
            pltpu.VMEM((ITERS, 6, 128), F32),
            pltpu.VMEM((ITERS, 63, 6, 128), F32),
            pltpu.VMEM((2, 6, 128), F32),
            pltpu.VMEM((2, 7, 6, 128), F32),
            pltpu.VMEM((8, 128), F32),
            pltpu.VMEM((ROWS, D), F32),
            pltpu.VMEM((ROWS, D), F32),
            pltpu.VMEM((ROWS, D), BF16),
            pltpu.VMEM((2, 7, CHUNK, D), BF16),
            pltpu.VMEM((2, NX, 8, D), F32),
            pltpu.VMEM((2, 7, 8, D), F32),
            pltpu.VMEM((2, 8, D), F32),
            pltpu.VMEM((512, D), F32),
            pltpu.VMEM((512, D), BF16),
            pltpu.VMEM((512, D), BF16),
            pltpu.VMEM((8, 64, D), BF16),
            pltpu.VMEM((8, 64, D), BF16),
            dma((8,)),
            dma((8,)),
            dma((ITERS,)),
            dma((ITERS,)),
            dma((ITERS,)),
            dma((ITERS,)),
            dma((2,)),
            dma((2,)),
            dma((6,)),
            dma((6,)),
        ],
        compiler_params=pltpu.CompilerParams(
            collective_id=0, has_side_effects=True, vmem_limit_bytes=40 * 1024 * 1024
        ),
    )(*(pltpu.with_memory_space_constraint(a, pltpu.HBM) for a in arguments))


def solution(mesh):
    return jax.shard_map(
        on_device,
        mesh=mesh,
        in_specs=(
            P(("dp", "proto"), None),
            P(("dp", "proto"), None),
            P("proto", None),
            P("proto", None),
            P(),
        ),
        out_specs=(P(("dp", "proto"), None), P("proto", "dp", None)),
        check_vma=False,
    )
```

```python
import jax
import jax.numpy as jnp
from jax import lax
from jax.experimental import pallas as pl
from jax.experimental.pallas import tpu as pltpu
from jax.sharding import PartitionSpec as P

MESH = pl.DeviceIdType.MESH
F32 = jnp.float32
BF16 = jnp.bfloat16

ITERS = 3
EPS = 1e-06
NX = 8
SLOT = 12
HALF = 6
CHUNK = NX * HALF
ROWS = 768
PROTOS = 1024
D = 256
NT = (((1,), (1,)), ((), ()))
TN = (((0,), (0,)), ((), ()))
FAR_FIRST = (4, 3, 5, 2, 6, 1, 7)


def hops(k):
    return min(k % NX, NX - k % NX) + min(k // NX, NX - k // NX)


PLANE = sorted(range(1, NX * NX), key=lambda k: -hops(k))


def unit_rows(values):
    widened = values.astype(F32)
    length = jnp.sqrt(jnp.sum(widened * widened, axis=1, keepdims=True) + EPS)
    return widened * (1.0 / length), length


def slot_row(index):
    first = index + HALF * ((index * 10923) >> 16)
    rest = index - ROWS // 2
    block = (rest * 1366) >> 16
    inner = rest - block * CHUNK
    six = (inner * 43) >> 8
    second = six * (NX * SLOT) + block * SLOT + HALF + inner - six * HALF
    return jnp.where(index < ROWS // 2, first, second)


def kernel(
    sf_hbm, tf_hbm, pr_hbm, tp_hbm, lc_hbm, out_s, out_p,
    sf, tf, pr, tp, lc, isem,
    stage, msg, g1, trow, srow, tpb, prb, wt, ex, gr, ub, ab,
    cs, cr, rs, rr, ps, pg, vv,
    pull, pullw, pullb, q1, q2s, q2, sixes, push, pushb, sib, zsend, zrecv,
    gsend, grecv, csend, crecv, rsend, rrecv, psend, precv, fsend, frecv,
):
    d = lax.axis_index("dp")
    p = lax.axis_index("proto")
    y, x = p // NX, p % NX
    z, c = d // 2, d % 2

    def xp(k):
        return (d, y * NX + (x + k) % NX)

    def yp(k):
        return (d, ((y + k) % NX) * NX + x)

    def plane(k):
        return (d, ((y + k // NX) % NX) * NX + (x + k % NX) % NX)

    def dpp(k):
        return ((d + k) % 16, p)

    def send(src, dst, ssem, rsem, dev):
        pltpu.make_async_remote_copy(
            src_ref=src, dst_ref=dst, send_sem=ssem, recv_sem=rsem, device_id=dev, device_id_type=MESH
        ).start()

    def wait(ref, sem):
        pltpu.make_async_copy(ref, ref, sem).wait()

    barrier = pltpu.get_barrier_semaphore()
    for k in FAR_FIRST:
        pl.semaphore_signal(barrier, inc=1, device_id=xp(k), device_id_type=MESH)
        pl.semaphore_signal(barrier, inc=1, device_id=yp(k), device_id_type=MESH)
    for k in range(1, 16):
        pl.semaphore_signal(barrier, inc=1, device_id=dpp(k), device_id_type=MESH)

    inputs = ((tf_hbm, tf), (sf_hbm, sf), (lc_hbm, lc), (tp_hbm, tp), (pr_hbm, pr))
    for i, (src, dst) in enumerate(inputs):
        pltpu.make_async_copy(src, dst, isem.at[i]).start()

    def arrived(i):
        pltpu.make_async_copy(*inputs[i], isem.at[i]).wait()

    arrived(0)
    arrived(1)
    su, _ = unit_rows(sf[...])
    tu, _ = unit_rows(tf[...])
    stage[...] = jnp.zeros_like(stage)
    for kind, unit in enumerate((tu, su)):
        for half in range(2):
            six = unit[half * HALF : half * HALF + HALF]
            stage[kind, half, 0:HALF] = six[:, 0:128]
            stage[kind, half, HALF:SLOT] = six[:, 128:D]
    msg[...] = stage[...].astype(BF16)
    for kind in range(2):
        g1[kind, 0, x] = msg[kind, 0]
        g1[kind, 1, y] = msg[kind, 1]
    pl.semaphore_wait(barrier, 2 * (NX - 1) + 15)
    for kind in range(2):
        for k in FAR_FIRST:
            for half, at, peer in ((0, x, xp), (1, y, yp)):
                send(
                    msg.at[kind, half], g1.at[kind, half, at],
                    gsend.at[kind * 2 + half], grecv.at[kind * 2 + half], peer(k),
                )

    def unit_protos(i, carry):
        rows = pl.ds(pl.multiple_of(i * 128, 128), 128)
        tpb[rows, :] = unit_rows(tp[rows, :])[0].astype(BF16)
        prb[rows, :] = unit_rows(pr[rows, :])[0].astype(BF16)
        return carry

    arrived(3)
    arrived(4)
    lax.fori_loop(0, PROTOS // 128, unit_protos, 0)
    arrived(2)
    live = lc[d]
    ub[...] = (slot_row(lax.broadcasted_iota(jnp.int32, (ROWS, 128), 0)) < live).astype(F32)
    flat = lax.broadcasted_iota(jnp.int32, (6, 128), 0) * 128 + lax.broadcasted_iota(jnp.int32, (6, 128), 1)
    live_flat = slot_row(flat) < live

    ri = lax.broadcasted_iota(jnp.int32, (2 * CHUNK, NX * 16), 0)
    ci = lax.broadcasted_iota(jnp.int32, (2 * CHUNK, NX * 16), 1)
    inner = jnp.where(ri < CHUNK, ri, ri - CHUNK)
    six = (inner * 43) >> 8
    source = six * 16 + (inner - six * HALF) + jnp.where(ri < CHUNK, 0, HALF)
    pick = (ci == source).astype(F32).astype(BF16)
    first = pl.ds(pl.multiple_of(y * CHUNK, CHUNK), CHUNK)
    second = pl.ds(pl.multiple_of(ROWS // 2 + x * CHUNK, CHUNK), CHUNK)

    def assemble(kind, rows_ref):
        for half, place in ((0, first), (1, second)):
            wait(g1.at[kind, half, pl.ds(0, NX - 1)], grecv.at[kind * 2 + half])
            picked = jnp.dot(pick, g1[kind, half].reshape(NX * 16, 128), preferred_element_type=F32).astype(BF16)
            rows_ref[place, 0:128] = picked[0:CHUNK]
            rows_ref[place, 128:D] = picked[CHUNK:]
            if kind == 0:
                second_gather(kind, rows_ref, half)

    def second_gather(kind, rows_ref, half):
        place, peer = ((first, yp), (second, xp))[half]
        for k in FAR_FIRST:
            sem = 4 + kind * 2 + half
            send(rows_ref.at[place], rows_ref.at[place], gsend.at[sem], grecv.at[sem], peer(k))

    assemble(0, trow)
    assemble(1, srow)

    def scores(rows_ref, protos_ref, out_ref, scale, weighted=False):
        parts = []
        for n in range(4):
            acc = jnp.zeros((8, 256), F32)
            for m in range(3):
                rows, cols = pl.ds(m * 256, 256), pl.ds(n * 256, 256)
                s = lax.dot_general(rows_ref[rows, :], protos_ref[cols, :], NT, preferred_element_type=F32)
                e = jnp.exp(s * scale)
                out_ref[rows, cols] = e
                if weighted:
                    u = jnp.concatenate([ub[rows, :]] * 2, axis=1)
                    acc = acc + jnp.sum((e * u).reshape(32, 8, 256), axis=0)
            parts.append(acc)
        return jnp.concatenate(parts, axis=1)

    wait(trow.at[pl.ds(0, 7 * CHUNK)], grecv.at[4])
    wait(trow.at[pl.ds(0, 7 * CHUNK)], grecv.at[5])
    first_sums = scores(trow, tpb, wt, 1.0 / 0.07, True)

    def column_pass(it):
        def body(i, acc):
            rows = pl.ds(pl.multiple_of(i * 32, 32), 32)
            w = wt[rows, :]
            u = ub[rows, :]
            for t in range(4):
                ut = jnp.concatenate([u[t * 8 : t * 8 + 8]] * 8, axis=1)
                acc = acc + w[t * 8 : t * 8 + 8] * ut
            return acc

        if it == 0:
            acc = first_sums
        else:
            acc = lax.fori_loop(0, ROWS // 32, body, jnp.zeros((8, PROTOS), F32), unroll=4)
        total = jnp.sum(acc, axis=0, keepdims=True)
        for n in range(8):
            cs[it, n : n + 1, :] = total[:, n * 128 : n * 128 + 128]
        for k in (8, 7, 9, 6, 10, 5, 11, 4, 12, 3, 13, 2, 14, 1, 15):
            send(cs.at[it], cr.at[it, k - 1], csend.at[it], crecv.at[it], dpp(k))

    def column_wait(it):
        wait(cr.at[it], crecv.at[it])
        vv[...] = 1.0 / (cs[it] + jnp.sum(cr[it], axis=0))

    def lane_sums(src_ref, weights, out_ref):
        for n in range(6):
            rows = pl.ds(n * 128, 128)
            acc = jnp.zeros((128, 128), F32)
            for t in range(8):
                acc = acc + src_ref[rows, pl.ds(t * 128, 128)] * weights[t : t + 1, :]
            out_ref[n : n + 1, :] = jnp.sum(acc.T, axis=0, keepdims=True)

    def spread(flat_rows, out_ref):
        for n in range(6):
            out_ref[pl.ds(n * 128, 128), :] = jnp.broadcast_to(flat_rows[n : n + 1, :], (128, 128)).T

    def proto_send(src, dst, ssem, rsem, axis):
        for k in FAR_FIRST:
            send(src.at[axis], dst.at[axis, k - 1], ssem.at[axis], rsem.at[axis], (xp, yp)[axis](k))

    def proto_sum(src, dst, rsem, axis):
        wait(dst.at[axis], rsem.at[axis])
        return src[axis] + jnp.sum(dst[axis], axis=0)

    def inverse(total):
        return jnp.where(live_flat, 1.0 / jnp.where(live_flat, total, 1.0), 0.0)

    for it in range(ITERS):
        column_pass(it)
        if it == 0:
            second_gather(1, srow, 0)
            second_gather(1, srow, 1)
        if it == 1:
            wait(srow.at[pl.ds(0, 7 * CHUNK)], grecv.at[6])
            wait(srow.at[pl.ds(0, 7 * CHUNK)], grecv.at[7])
            scores(srow, prb, ex, 10.0)
            lane_sums(ex, jnp.ones((8, 128), F32), ps.at[0])
            proto_send(ps, pg, psend, precv, 0)
        if it == 2:
            ps[1] = proto_sum(ps, pg, precv, 0)
            proto_send(ps, pg, psend, precv, 1)
        column_wait(it)
        lane_sums(wt, vv[...], rs.at[it])
        for k in PLANE:
            send(rs.at[it], rr.at[it, k - 1], rsend.at[it], rrecv.at[it], plane(k))
        if it == 2:
            partition = proto_sum(ps, pg, precv, 1)
            spread(10.0 * inverse(partition), ab)

            v_row = jnp.concatenate([vv[n : n + 1, :] for n in range(8)], axis=1)

            def by_protos(values):
                high = values.astype(BF16)
                low = (values - high.astype(F32)).astype(BF16)
                return jnp.dot(high, prb[...], preferred_element_type=F32) + jnp.dot(
                    low, prb[...], preferred_element_type=F32
                )

            def fold(i, carry):
                rows = pl.ds(pl.multiple_of(i * 128, 128), 128)
                e = ex[rows, :] * jnp.concatenate([ab[rows, :]] * 8, axis=1)
                ex[rows, :] = e
                pull[rows, :] = by_protos(e)
                w = wt[rows, :] * v_row
                wt[rows, :] = w
                pullw[rows, :] = by_protos(w)
                return carry

            lax.fori_loop(0, ROWS // 128, fold, 0)
        wait(rr.at[it], rrecv.at[it])
        total = rs[it] + jnp.sum(rr[it], axis=0)
        spread(inverse(total) * (10.0 if it == ITERS - 1 else 1.0), ub)

    def finish(i, carry):
        rows = pl.ds(pl.multiple_of(i * 48, 48), 48)
        u = jnp.concatenate([ub[rows, :]] * 2, axis=1)
        part = pull[rows, :] - pullw[rows, :] * u
        pull[rows, :] = part
        pullb[rows, :] = part.astype(BF16)
        return carry

    lax.fori_loop(0, ROWS // 48, finish, 0, unroll=2)
    for k in FAR_FIRST:
        to_y = pl.ds(pl.multiple_of(((y + k) % NX) * CHUNK, CHUNK), CHUNK)
        to_x = pl.ds(pl.multiple_of(ROWS // 2 + ((x + k) % NX) * CHUNK, CHUNK), CHUNK)
        send(pullb.at[to_y], q1.at[0, k - 1], fsend.at[0], frecv.at[0], yp(k))
        send(pullb.at[to_x], q1.at[1, k - 1], fsend.at[1], frecv.at[1], xp(k))

    other = pl.ds(pl.multiple_of((1 - c) * 512, 512), 512)
    mine = pl.ds(pl.multiple_of(c * 512, 512), 512)

    def grads(first):
        def body(i, carry):
            rows = pl.ds(pl.multiple_of(i * 32, 32), 32)
            u = ub[rows, :]
            for n in range(4):
                cols = pl.ds(pl.multiple_of(first + n * 128, 128), 128)
                gr[rows, cols] = (ex[rows, cols] - wt[rows, cols] * u).astype(BF16)
            return carry

        lax.fori_loop(0, ROWS // 32, body, 0, unroll=2)

    grads((1 - c) * 512)
    pushb[...] = lax.dot_general(gr[:, other], srow[...], TN, preferred_element_type=F32).astype(BF16)
    send(pushb, sib, fsend.at[2], frecv.at[2], (z * 2 + 1 - c, p))
    grads(c * 512)
    push[...] = lax.dot_general(gr[:, mine], srow[...], TN, preferred_element_type=F32)
    wait(sib, frecv.at[2])
    zsend[...] = (push[...] + sib[...].astype(F32)).astype(BF16).reshape(8, 64, D)
    keeps = c == z // 4
    for k in FAR_FIRST + (0,):
        for core in range(2):
            to = ((z + k) % NX) * 2 + core

            @pl.when((to // 8 == c) & (to != d))
            def _(to=to):
                send(zsend.at[to - 8 * c], zrecv.at[z], fsend.at[3], frecv.at[3], (to, p))

    @pl.when(keeps)
    def _():
        zrecv[z] = zsend[d - 8 * c]

    for half, own, peer in ((0, first, xp), (1, second, yp)):
        wait(q1.at[half], frecv.at[half])
        total = pull[own, :] + jnp.sum(q1[half].astype(F32), axis=0)
        for n in range(NX):
            q2s[half, n, 0:HALF] = total[n * HALF : n * HALF + HALF]
            q2s[half, n, HALF:8] = jnp.zeros((8 - HALF, D), F32)
        at = x if half == 0 else y
        for k in FAR_FIRST:
            send(q2s.at[half, (at + k) % NX], q2.at[half, k - 1], fsend.at[4 + half], frecv.at[4 + half], peer(k))

    own_rows = pl.ds(pl.multiple_of(d * 64, 64), 64)
    proto_unit, proto_length = unit_rows(pr[own_rows, :])

    @pl.when(keeps)
    def _():
        wait(zrecv.at[pl.ds(0, 7)], frecv.at[3])
        wait(zrecv.at[pl.ds(0, 7)], fsend.at[3])

    @pl.when(jnp.logical_not(keeps))
    def _():
        wait(zrecv, frecv.at[3])
        wait(zrecv, fsend.at[3])

    pushed = jnp.sum(zrecv[...].astype(F32), axis=0)
    out_p[0] = (pushed - proto_unit * jnp.sum(proto_unit * pushed, axis=1, keepdims=True)) * (1.0 / proto_length)

    student_unit, student_length = unit_rows(sf[...])
    for half in range(2):
        wait(q2.at[half], frecv.at[4 + half])
        at = x if half == 0 else y
        sixes[half] = q2s[half, at] + jnp.sum(q2[half], axis=0)
    pulled = jnp.concatenate([sixes[0, 0:HALF], sixes[1, 0:HALF]], axis=0)
    out_s[...] = (pulled - student_unit * jnp.sum(student_unit * pulled, axis=1, keepdims=True)) * (1.0 / student_length)

    for half in range(2):
        for kind, rows_ref in enumerate((trow, srow)):
            wait(g1.at[kind, half, pl.ds(0, NX - 1)], gsend.at[kind * 2 + half])
            wait(rows_ref.at[pl.ds(0, 7 * CHUNK)], gsend.at[4 + kind * 2 + half])
        wait(pg.at[half], psend.at[half])
        wait(q1.at[half], fsend.at[half])
        wait(q2.at[half], fsend.at[4 + half])
    for it in range(ITERS):
        wait(rr.at[it], rsend.at[it])
        wait(cr.at[it], csend.at[it])
    wait(sib, fsend.at[2])


def on_device(*arguments):
    vmem = pl.BlockSpec(memory_space=pltpu.VMEM)
    dma = pltpu.SemaphoreType.DMA
    return pl.pallas_call(
        kernel,
        out_shape=(
            jax.ShapeDtypeStruct((SLOT, D), F32),
            jax.ShapeDtypeStruct((1, PROTOS // 16, D), F32),
        ),
        in_specs=[pl.BlockSpec(memory_space=pltpu.HBM)] * 5,
        out_specs=(vmem, vmem),
        scratch_shapes=[
            pltpu.VMEM((SLOT, D), BF16),
            pltpu.VMEM((SLOT, D), BF16),
            pltpu.VMEM((PROTOS, D), BF16),
            pltpu.VMEM((PROTOS, D), BF16),
            pltpu.SMEM((16,), jnp.int32),
            dma((5,)),
            pltpu.VMEM((2, 2, 16, 128), F32),
            pltpu.VMEM((2, 2, 16, 128), BF16),
            pltpu.VMEM((2, 2, NX, 16, 128), BF16),
            pltpu.VMEM((ROWS, D), BF16),
            pltpu.VMEM((ROWS, D), BF16),
            pltpu.VMEM((PROTOS, D), BF16),
            pltpu.VMEM((PROTOS, D), BF16),
            pltpu.VMEM((ROWS, PROTOS), F32),
            pltpu.VMEM((ROWS, PROTOS), F32),
            pltpu.VMEM((ROWS, PROTOS), BF16),
            pltpu.VMEM((ROWS, 128), F32),
            pltpu.VMEM((ROWS, 128), F32),
            pltpu.VMEM((ITERS, 8, 128), F32),
            pltpu.VMEM((ITERS, 15, 8, 128), F32),
            pltpu.VMEM((ITERS, 6, 128), F32),
            pltpu.VMEM((ITERS, 63, 6, 128), F32),
            pltpu.VMEM((2, 6, 128), F32),
            pltpu.VMEM((2, 7, 6, 128), F32),
            pltpu.VMEM((8, 128), F32),
            pltpu.VMEM((ROWS, D), F32),
            pltpu.VMEM((ROWS, D), F32),
            pltpu.VMEM((ROWS, D), BF16),
            pltpu.VMEM((2, 7, CHUNK, D), BF16),
            pltpu.VMEM((2, NX, 8, D), F32),
            pltpu.VMEM((2, 7, 8, D), F32),
            pltpu.VMEM((2, 8, D), F32),
            pltpu.VMEM((512, D), F32),
            pltpu.VMEM((512, D), BF16),
            pltpu.VMEM((512, D), BF16),
            pltpu.VMEM((8, 64, D), BF16),
            pltpu.VMEM((8, 64, D), BF16),
            dma((8,)),
            dma((8,)),
            dma((ITERS,)),
            dma((ITERS,)),
            dma((ITERS,)),
            dma((ITERS,)),
            dma((2,)),
            dma((2,)),
            dma((6,)),
            dma((6,)),
        ],
        compiler_params=pltpu.CompilerParams(
            collective_id=0, has_side_effects=True, vmem_limit_bytes=40 * 1024 * 1024
        ),
    )(*(pltpu.with_memory_space_constraint(a, pltpu.HBM) for a in arguments))


def solution(mesh):
    return jax.shard_map(
        on_device,
        mesh=mesh,
        in_specs=(
            P(("dp", "proto"), None),
            P(("dp", "proto"), None),
            P("proto", None),
            P("proto", None),
            P(),
        ),
        out_specs=(P(("dp", "proto"), None), P("proto", "dp", None)),
        check_vma=False,
    )
```

```python
import jax
import jax.numpy as jnp
from jax import lax
from jax.experimental import pallas as pl
from jax.experimental.pallas import tpu as pltpu
from jax.sharding import PartitionSpec as P

MESH = pl.DeviceIdType.MESH
F32 = jnp.float32
BF16 = jnp.bfloat16

ITERS = 3
EPS = 1e-06
NX = 8
SLOT = 12
HALF = 6
CHUNK = NX * HALF
ROWS = 768
PROTOS = 1024
D = 256
NT = (((1,), (1,)), ((), ()))
TN = (((0,), (0,)), ((), ()))
FAR_FIRST = (4, 3, 5, 2, 6, 1, 7)


def hops(k):
    return min(k % NX, NX - k % NX) + min(k // NX, NX - k // NX)


PLANE = sorted(range(1, NX * NX), key=lambda k: -hops(k))


def unit_rows(values):
    widened = values.astype(F32)
    length = jnp.sqrt(jnp.sum(widened * widened, axis=1, keepdims=True) + EPS)
    return widened * (1.0 / length), length


def slot_row(index):
    first = index + HALF * ((index * 10923) >> 16)
    rest = index - ROWS // 2
    block = (rest * 1366) >> 16
    inner = rest - block * CHUNK
    six = (inner * 43) >> 8
    second = six * (NX * SLOT) + block * SLOT + HALF + inner - six * HALF
    return jnp.where(index < ROWS // 2, first, second)


def kernel(
    sf_hbm, tf_hbm, pr_hbm, tp_hbm, lc_hbm, out_s, out_p,
    sf, tf, pr, tp, lc, isem,
    stage, msg, g1, trow, srow, tpb, prb, wt, ex, gr, ub, ab,
    cs, cr, rs, rr, ps, pg, vv,
    pull, pullw, pullb, q1, q2s, q2, sixes, push, pushb, sib, zsend, zrecv,
    gsend, grecv, csend, crecv, rsend, rrecv, psend, precv, fsend, frecv,
):
    d = lax.axis_index("dp")
    p = lax.axis_index("proto")
    y, x = p // NX, p % NX
    z, c = d // 2, d % 2

    def xp(k):
        return (d, y * NX + (x + k) % NX)

    def yp(k):
        return (d, ((y + k) % NX) * NX + x)

    def plane(k):
        return (d, ((y + k // NX) % NX) * NX + (x + k % NX) % NX)

    def dpp(k):
        return ((d + k) % 16, p)

    def send(src, dst, ssem, rsem, dev):
        pltpu.make_async_remote_copy(
            src_ref=src, dst_ref=dst, send_sem=ssem, recv_sem=rsem, device_id=dev, device_id_type=MESH
        ).start()

    def wait(ref, sem):
        pltpu.make_async_copy(ref, ref, sem).wait()

    barrier = pltpu.get_barrier_semaphore()
    for k in FAR_FIRST:
        pl.semaphore_signal(barrier, inc=1, device_id=xp(k), device_id_type=MESH)
        pl.semaphore_signal(barrier, inc=1, device_id=yp(k), device_id_type=MESH)
    for k in range(1, 16):
        pl.semaphore_signal(barrier, inc=1, device_id=dpp(k), device_id_type=MESH)

    inputs = ((tf_hbm, tf), (sf_hbm, sf), (lc_hbm, lc), (tp_hbm, tp), (pr_hbm, pr))
    for i, (src, dst) in enumerate(inputs):
        pltpu.make_async_copy(src, dst, isem.at[i]).start()

    def arrived(i):
        pltpu.make_async_copy(*inputs[i], isem.at[i]).wait()

    arrived(0)
    arrived(1)
    su, _ = unit_rows(sf[...])
    tu, _ = unit_rows(tf[...])
    stage[...] = jnp.zeros_like(stage)
    for kind, unit in enumerate((tu, su)):
        for half in range(2):
            six = unit[half * HALF : half * HALF + HALF]
            stage[kind, half, 0:HALF] = six[:, 0:128]
            stage[kind, half, HALF:SLOT] = six[:, 128:D]
    msg[...] = stage[...].astype(BF16)
    for kind in range(2):
        g1[kind, 0, x] = msg[kind, 0]
        g1[kind, 1, y] = msg[kind, 1]
    pl.semaphore_wait(barrier, 2 * (NX - 1) + 15)
    for kind in range(2):
        for k in FAR_FIRST:
            for half, at, peer in ((0, x, xp), (1, y, yp)):
                send(
                    msg.at[kind, half], g1.at[kind, half, at],
                    gsend.at[kind * 2 + half], grecv.at[kind * 2 + half], peer(k),
                )

    def unit_protos(i, carry):
        rows = pl.ds(pl.multiple_of(i * 128, 128), 128)
        tpb[rows, :] = unit_rows(tp[rows, :])[0].astype(BF16)
        prb[rows, :] = unit_rows(pr[rows, :])[0].astype(BF16)
        return carry

    arrived(3)
    arrived(4)
    lax.fori_loop(0, PROTOS // 128, unit_protos, 0)
    arrived(2)
    live = lc[d]
    ub[...] = (slot_row(lax.broadcasted_iota(jnp.int32, (ROWS, 128), 0)) < live).astype(F32)
    flat = lax.broadcasted_iota(jnp.int32, (6, 128), 0) * 128 + lax.broadcasted_iota(jnp.int32, (6, 128), 1)
    live_flat = slot_row(flat) < live

    ri = lax.broadcasted_iota(jnp.int32, (2 * CHUNK, NX * 16), 0)
    ci = lax.broadcasted_iota(jnp.int32, (2 * CHUNK, NX * 16), 1)
    inner = jnp.where(ri < CHUNK, ri, ri - CHUNK)
    six = (inner * 43) >> 8
    source = six * 16 + (inner - six * HALF) + jnp.where(ri < CHUNK, 0, HALF)
    pick = (ci == source).astype(F32).astype(BF16)
    first = pl.ds(pl.multiple_of(y * CHUNK, CHUNK), CHUNK)
    second = pl.ds(pl.multiple_of(ROWS // 2 + x * CHUNK, CHUNK), CHUNK)

    def assemble(kind, rows_ref):
        for half, place in ((0, first), (1, second)):
            wait(g1.at[kind, half, pl.ds(0, NX - 1)], grecv.at[kind * 2 + half])
            picked = jnp.dot(pick, g1[kind, half].reshape(NX * 16, 128), preferred_element_type=F32).astype(BF16)
            rows_ref[place, 0:128] = picked[0:CHUNK]
            rows_ref[place, 128:D] = picked[CHUNK:]
            if kind == 0:
                second_gather(kind, rows_ref, half)

    def second_gather(kind, rows_ref, half):
        place, peer = ((first, yp), (second, xp))[half]
        for k in FAR_FIRST:
            sem = 4 + kind * 2 + half
            send(rows_ref.at[place], rows_ref.at[place], gsend.at[sem], grecv.at[sem], peer(k))

    assemble(0, trow)
    assemble(1, srow)

    def scores(rows_ref, protos_ref, out_ref, scale, weighted=False):
        parts = []
        for n in range(4):
            acc = jnp.zeros((8, 256), F32)
            for m in range(3):
                rows, cols = pl.ds(m * 256, 256), pl.ds(n * 256, 256)
                s = lax.dot_general(rows_ref[rows, :], protos_ref[cols, :], NT, preferred_element_type=F32)
                e = jnp.exp(s * scale)
                out_ref[rows, cols] = e
                if weighted:
                    u = jnp.concatenate([ub[rows, :]] * 2, axis=1)
                    acc = acc + jnp.sum((e * u).reshape(32, 8, 256), axis=0)
            parts.append(acc)
        return jnp.concatenate(parts, axis=1)

    wait(trow.at[pl.ds(0, 7 * CHUNK)], grecv.at[4])
    wait(trow.at[pl.ds(0, 7 * CHUNK)], grecv.at[5])
    first_sums = scores(trow, tpb, wt, 1.0 / 0.07, True)

    def column_pass(it):
        def body(i, acc):
            rows = pl.ds(pl.multiple_of(i * 32, 32), 32)
            w = wt[rows, :]
            u = ub[rows, :]
            for t in range(4):
                ut = jnp.concatenate([u[t * 8 : t * 8 + 8]] * 8, axis=1)
                acc = acc + w[t * 8 : t * 8 + 8] * ut
            return acc

        if it == 0:
            acc = first_sums
        else:
            acc = lax.fori_loop(0, ROWS // 32, body, jnp.zeros((8, PROTOS), F32), unroll=4)
        total = jnp.sum(acc, axis=0, keepdims=True)
        for n in range(8):
            cs[it, n : n + 1, :] = total[:, n * 128 : n * 128 + 128]
        for k in (8, 7, 9, 6, 10, 5, 11, 4, 12, 3, 13, 2, 14, 1, 15):
            send(cs.at[it], cr.at[it, k - 1], csend.at[it], crecv.at[it], dpp(k))

    def column_wait(it):
        wait(cr.at[it], crecv.at[it])
        vv[...] = 1.0 / (cs[it] + jnp.sum(cr[it], axis=0))

    def lane_sums(src_ref, weights, out_ref):
        for n in range(6):
            rows = pl.ds(n * 128, 128)
            acc = jnp.zeros((128, 128), F32)
            for t in range(8):
                acc = acc + src_ref[rows, pl.ds(t * 128, 128)] * weights[t : t + 1, :]
            out_ref[n : n + 1, :] = jnp.sum(acc.T, axis=0, keepdims=True)

    def spread(flat_rows, out_ref):
        for n in range(6):
            out_ref[pl.ds(n * 128, 128), :] = jnp.broadcast_to(flat_rows[n : n + 1, :], (128, 128)).T

    def proto_send(src, dst, ssem, rsem, axis):
        for k in FAR_FIRST:
            send(src.at[axis], dst.at[axis, k - 1], ssem.at[axis], rsem.at[axis], (xp, yp)[axis](k))

    def proto_sum(src, dst, rsem, axis):
        wait(dst.at[axis], rsem.at[axis])
        return src[axis] + jnp.sum(dst[axis], axis=0)

    def inverse(total):
        return jnp.where(live_flat, 1.0 / jnp.where(live_flat, total, 1.0), 0.0)

    for it in range(ITERS):
        column_pass(it)
        if it == 0:
            second_gather(1, srow, 0)
            second_gather(1, srow, 1)
        if it == 1:
            wait(srow.at[pl.ds(0, 7 * CHUNK)], grecv.at[6])
            wait(srow.at[pl.ds(0, 7 * CHUNK)], grecv.at[7])
            scores(srow, prb, ex, 10.0)
            lane_sums(ex, jnp.ones((8, 128), F32), ps.at[0])
            proto_send(ps, pg, psend, precv, 0)
        if it == 2:
            ps[1] = proto_sum(ps, pg, precv, 0)
            proto_send(ps, pg, psend, precv, 1)
        column_wait(it)
        lane_sums(wt, vv[...], rs.at[it])
        for k in PLANE:
            send(rs.at[it], rr.at[it, k - 1], rsend.at[it], rrecv.at[it], plane(k))
        if it == 2:
            partition = proto_sum(ps, pg, precv, 1)
            spread(10.0 * inverse(partition), ab)

            v_row = jnp.concatenate([vv[n : n + 1, :] for n in range(8)], axis=1)

            def by_protos(values):
                high = values.astype(BF16)
                low = (values - high.astype(F32)).astype(BF16)
                return jnp.dot(high, prb[...], preferred_element_type=F32) + jnp.dot(
                    low, prb[...], preferred_element_type=F32
                )

            def fold(i, carry):
                rows = pl.ds(pl.multiple_of(i * 128, 128), 128)
                e = ex[rows, :] * jnp.concatenate([ab[rows, :]] * 8, axis=1)
                ex[rows, :] = e
                pull[rows, :] = by_protos(e)
                w = wt[rows, :] * v_row
                wt[rows, :] = w
                pullw[rows, :] = by_protos(w)
                return carry

            lax.fori_loop(0, ROWS // 128, fold, 0)
        wait(rr.at[it], rrecv.at[it])
        total = rs[it] + jnp.sum(rr[it], axis=0)
        spread(inverse(total) * (10.0 if it == ITERS - 1 else 1.0), ub)

    def finish(i, carry):
        rows = pl.ds(pl.multiple_of(i * 48, 48), 48)
        u = jnp.concatenate([ub[rows, :]] * 2, axis=1)
        part = pull[rows, :] - pullw[rows, :] * u
        pull[rows, :] = part
        pullb[rows, :] = part.astype(BF16)
        return carry

    lax.fori_loop(0, ROWS // 48, finish, 0, unroll=2)
    for k in FAR_FIRST:
        to_y = pl.ds(pl.multiple_of(((y + k) % NX) * CHUNK, CHUNK), CHUNK)
        to_x = pl.ds(pl.multiple_of(ROWS // 2 + ((x + k) % NX) * CHUNK, CHUNK), CHUNK)
        send(pullb.at[to_y], q1.at[0, k - 1], fsend.at[0], frecv.at[0], yp(k))
        send(pullb.at[to_x], q1.at[1, k - 1], fsend.at[1], frecv.at[1], xp(k))

    other = pl.ds(pl.multiple_of((1 - c) * 512, 512), 512)
    mine = pl.ds(pl.multiple_of(c * 512, 512), 512)

    def grads(first):
        def body(i, carry):
            rows = pl.ds(pl.multiple_of(i * 32, 32), 32)
            u = ub[rows, :]
            for n in range(4):
                cols = pl.ds(pl.multiple_of(first + n * 128, 128), 128)
                gr[rows, cols] = (ex[rows, cols] - wt[rows, cols] * u).astype(BF16)
            return carry

        lax.fori_loop(0, ROWS // 32, body, 0, unroll=2)

    grads((1 - c) * 512)
    pushb[...] = lax.dot_general(gr[:, other], srow[...], TN, preferred_element_type=F32).astype(BF16)
    send(pushb, sib, fsend.at[2], frecv.at[2], (z * 2 + 1 - c, p))
    grads(c * 512)
    push[...] = lax.dot_general(gr[:, mine], srow[...], TN, preferred_element_type=F32)
    wait(sib, frecv.at[2])
    zsend[...] = (push[...] + sib[...].astype(F32)).astype(BF16).reshape(8, 64, D)
    keeps = c == z // 4
    for k in FAR_FIRST + (0,):
        for core in range(2):
            to = ((z + k) % NX) * 2 + core

            @pl.when((to // 8 == c) & (to != d))
            def _(to=to):
                send(zsend.at[to - 8 * c], zrecv.at[z], fsend.at[3], frecv.at[3], (to, p))

    @pl.when(keeps)
    def _():
        zrecv[z] = zsend[d - 8 * c]

    for half, own, peer in ((0, first, xp), (1, second, yp)):
        wait(q1.at[half], frecv.at[half])
        total = pull[own, :] + jnp.sum(q1[half].astype(F32), axis=0)
        for n in range(NX):
            q2s[half, n, 0:HALF] = total[n * HALF : n * HALF + HALF]
            q2s[half, n, HALF:8] = jnp.zeros((8 - HALF, D), F32)
        at = x if half == 0 else y
        for k in FAR_FIRST:
            send(q2s.at[half, (at + k) % NX], q2.at[half, k - 1], fsend.at[4 + half], frecv.at[4 + half], peer(k))

    own_rows = pl.ds(pl.multiple_of(d * 64, 64), 64)
    proto_unit, proto_length = unit_rows(pr[own_rows, :])

    @pl.when(keeps)
    def _():
        wait(zrecv.at[pl.ds(0, 7)], frecv.at[3])
        wait(zrecv.at[pl.ds(0, 7)], fsend.at[3])

    @pl.when(jnp.logical_not(keeps))
    def _():
        wait(zrecv, frecv.at[3])
        wait(zrecv, fsend.at[3])

    pushed = jnp.sum(zrecv[...].astype(F32), axis=0)
    out_p[0] = (pushed - proto_unit * jnp.sum(proto_unit * pushed, axis=1, keepdims=True)) * (1.0 / proto_length)

    student_unit, student_length = unit_rows(sf[...])
    for half in range(2):
        wait(q2.at[half], frecv.at[4 + half])
        at = x if half == 0 else y
        sixes[half] = q2s[half, at] + jnp.sum(q2[half], axis=0)
    pulled = jnp.concatenate([sixes[0, 0:HALF], sixes[1, 0:HALF]], axis=0)
    out_s[...] = (pulled - student_unit * jnp.sum(student_unit * pulled, axis=1, keepdims=True)) * (1.0 / student_length)

    for half in range(2):
        for kind, rows_ref in enumerate((trow, srow)):
            wait(g1.at[kind, half, pl.ds(0, NX - 1)], gsend.at[kind * 2 + half])
            wait(rows_ref.at[pl.ds(0, 7 * CHUNK)], gsend.at[4 + kind * 2 + half])
        wait(pg.at[half], psend.at[half])
        wait(q1.at[half], fsend.at[half])
        wait(q2.at[half], fsend.at[4 + half])
    for it in range(ITERS):
        wait(rr.at[it], rsend.at[it])
        wait(cr.at[it], csend.at[it])
    wait(sib, fsend.at[2])


def hand_out(rows, protos, out_s, out_p, sem):
    copies = (
        pltpu.make_async_copy(rows, out_s, sem.at[0]),
        pltpu.make_async_copy(protos, out_p, sem.at[1]),
    )
    for copy in copies:
        copy.start()
    for copy in copies:
        copy.wait()


def on_device(*arguments):
    vmem = pl.BlockSpec(memory_space=pltpu.VMEM)
    dma = pltpu.SemaphoreType.DMA
    grads = pl.pallas_call(
        kernel,
        out_shape=(
            jax.ShapeDtypeStruct((SLOT, D), F32),
            jax.ShapeDtypeStruct((1, PROTOS // 16, D), F32),
        ),
        in_specs=[pl.BlockSpec(memory_space=pltpu.HBM)] * 5,
        out_specs=(vmem, vmem),
        scratch_shapes=[
            pltpu.VMEM((SLOT, D), BF16),
            pltpu.VMEM((SLOT, D), BF16),
            pltpu.VMEM((PROTOS, D), BF16),
            pltpu.VMEM((PROTOS, D), BF16),
            pltpu.SMEM((16,), jnp.int32),
            dma((5,)),
            pltpu.VMEM((2, 2, 16, 128), F32),
            pltpu.VMEM((2, 2, 16, 128), BF16),
            pltpu.VMEM((2, 2, NX, 16, 128), BF16),
            pltpu.VMEM((ROWS, D), BF16),
            pltpu.VMEM((ROWS, D), BF16),
            pltpu.VMEM((PROTOS, D), BF16),
            pltpu.VMEM((PROTOS, D), BF16),
            pltpu.VMEM((ROWS, PROTOS), F32),
            pltpu.VMEM((ROWS, PROTOS), F32),
            pltpu.VMEM((ROWS, PROTOS), BF16),
            pltpu.VMEM((ROWS, 128), F32),
            pltpu.VMEM((ROWS, 128), F32),
            pltpu.VMEM((ITERS, 8, 128), F32),
            pltpu.VMEM((ITERS, 15, 8, 128), F32),
            pltpu.VMEM((ITERS, 6, 128), F32),
            pltpu.VMEM((ITERS, 63, 6, 128), F32),
            pltpu.VMEM((2, 6, 128), F32),
            pltpu.VMEM((2, 7, 6, 128), F32),
            pltpu.VMEM((8, 128), F32),
            pltpu.VMEM((ROWS, D), F32),
            pltpu.VMEM((ROWS, D), F32),
            pltpu.VMEM((ROWS, D), BF16),
            pltpu.VMEM((2, 7, CHUNK, D), BF16),
            pltpu.VMEM((2, NX, 8, D), F32),
            pltpu.VMEM((2, 7, 8, D), F32),
            pltpu.VMEM((2, 8, D), F32),
            pltpu.VMEM((512, D), F32),
            pltpu.VMEM((512, D), BF16),
            pltpu.VMEM((512, D), BF16),
            pltpu.VMEM((8, 64, D), BF16),
            pltpu.VMEM((8, 64, D), BF16),
            dma((8,)),
            dma((8,)),
            dma((ITERS,)),
            dma((ITERS,)),
            dma((ITERS,)),
            dma((ITERS,)),
            dma((2,)),
            dma((2,)),
            dma((6,)),
            dma((6,)),
        ],
        compiler_params=pltpu.CompilerParams(
            collective_id=0, has_side_effects=True, vmem_limit_bytes=40 * 1024 * 1024
        ),
    )(*(pltpu.with_memory_space_constraint(a, pltpu.HBM) for a in arguments))
    return pl.pallas_call(
        hand_out,
        out_shape=(
            jax.ShapeDtypeStruct((SLOT, D), F32),
            jax.ShapeDtypeStruct((1, PROTOS // 16, D), F32),
        ),
        in_specs=[vmem, vmem],
        compiler_params=pltpu.CompilerParams(vmem_limit_bytes=1024 * 1024),
        out_specs=(pl.BlockSpec(memory_space=pl.ANY),) * 2,
        scratch_shapes=[dma((2,))],
    )(*grads)


def solution(mesh):
    return jax.shard_map(
        on_device,
        mesh=mesh,
        in_specs=(
            P(("dp", "proto"), None),
            P(("dp", "proto"), None),
            P("proto", None),
            P("proto", None),
            P(),
        ),
        out_specs=(P(("dp", "proto"), None), P("proto", "dp", None)),
        check_vma=False,
    )
```
